32 devices in a mesh: row: 4 (over y, x), col: 8 (over z, core).
Axes of the slice: x: 2, y: 2, z: 4, core: 2. Of those that a mesh axis runs over, the one named last changes fastest.
Arguments:
- alignment_left: bfloat16 [512, 16384], P(('row', 'col')), may hold values from -6 to 6
- alignment_right: bfloat16 [512, 16384], P('row', 'col'), may hold values from -6 to 6
- pair_features: bfloat16 [512, 512, 128], P('row', 'col'), may hold values from -6 to 6
- output_weight: bfloat16 [1024, 128], replicated, may hold values from -4 to 4
- output_bias: float32 [128], replicated, may hold values from -4 to 4
- norm_scale_gain: float32 [128], replicated, may hold values from 0.1 to 1.9
- projection_weight: bfloat16 [128, 512], replicated, may hold values from -0.5 to 0.5
- gate_offset_bias: float32 [128], replicated, may hold values from -4 to 4
Outputs:
- new_pair: bfloat16 [512, 512, 128], P('row', 'col')
- projections: bfloat16 [512, 512, 512], P('row', 'col')
The draws below stay inside these ranges and needn't reach their ends.
All inputs are finite; a program needn't handle non-finite values.
Results may differ from the reference program's by a relative error of at most 0.0058.
Values may be sent and summed in bfloat16 or wider, within the bound.
No kernel may reach another device: no remote copies, remote signals or barrier semaphores. Data moves between devices by JAX's collectives and lax.ppermute only.
A program may use at most 192 MiB of HBM per device.

```python
import jax
import jax.numpy as jnp
from jax import lax

CHANNEL_WIDTH = 32
CZ = 128
HEADS = 4
DH = 32
ALIGNMENT_ROWS = 512
RESIDUE_COUNT = 512
PROJ = 512


def levels(rng, extent, split, low, largest):
    gain, own = 1.0, jax.random.fold_in(rng, 6)
    for dim, parts in split:
        steps = jnp.exp(jax.random.uniform(jax.random.fold_in(own, dim), (parts,), jnp.float32, low / len(split), largest / len(split)))
        gain = gain * jnp.repeat(steps, extent[dim] // parts).reshape([-1 if axis == dim else 1 for axis in range(len(extent))])
    return gain


def noise(rng, extent, scale, limit, pieces=(), dtype=jnp.bfloat16):
    result = scale * jax.random.normal(rng, extent, jnp.float32)
    if pieces:
        result = result * levels(rng, extent, pieces, -0.22, 0.18)
    return jnp.clip(result, -limit, limit).astype(dtype)


def setup_inputs(seed: int = 0) -> dict:
    splits = jax.random.split(jax.random.key(seed), 9)
    alignment_left = noise(splits[0], (RESIDUE_COUNT, CHANNEL_WIDTH * ALIGNMENT_ROWS), 1.0, 6.0, ((0, 32),))
    alignment_right = noise(splits[1], (ALIGNMENT_ROWS, RESIDUE_COUNT * CHANNEL_WIDTH), 1.0, 6.0, ((0, 4), (1, 8)))
    pair_features = noise(splits[2], (RESIDUE_COUNT, RESIDUE_COUNT, CZ), 1.0, 6.0, ((0, 4), (1, 8)))
    output_weight = noise(splits[3], (CHANNEL_WIDTH * CHANNEL_WIDTH, CZ), (CHANNEL_WIDTH * CHANNEL_WIDTH // ALIGNMENT_ROWS) ** -0.5, 4.0)
    output_bias = noise(splits[4], (CZ,), 1.0, 4.0, (), jnp.float32)
    norm_scale_gain = jnp.clip(1.0 + 0.18 * jax.random.normal(splits[5], (CZ,), jnp.float32), 0.1, 1.9)
    projection_weight = noise(splits[6], (CZ, PROJ), CZ ** -0.5, 0.5)
    gate_offset_bias = noise(splits[7], (HEADS * DH,), 1.0, 4.0, (), jnp.float32)
    return {"alignment_left": alignment_left, "alignment_right": alignment_right, "pair_features": pair_features, "output_weight": output_weight, "output_bias": output_bias, "norm_scale_gain": norm_scale_gain, "projection_weight": projection_weight, "gate_offset_bias": gate_offset_bias}


norm_eps = 1e-05

def project(values, norm_scale_gain, projection_weight, gate_offset_bias):
    widened = values.astype(jnp.float32)
    average = lax.optimization_barrier(jnp.mean(widened, axis=-1, keepdims=True))
    centred = widened - average
    variance = lax.optimization_barrier(jnp.mean(centred * centred, axis=-1, keepdims=True))
    normed = (centred * lax.rsqrt(variance + norm_eps) * norm_scale_gain).astype(jnp.bfloat16)
    projected = jnp.dot(normed, projection_weight, preferred_element_type=jnp.float32)
    quarter = projection_weight.shape[1] // 4
    head_part = projected[..., :3 * quarter]
    gate_part = jax.nn.sigmoid(projected[..., 3 * quarter:] + gate_offset_bias)
    return jnp.concatenate([head_part, gate_part], axis=-1).astype(jnp.bfloat16)

def reference(alignment_left, alignment_right, pair_features, output_weight, output_bias, norm_scale_gain, projection_weight, gate_offset_bias):
    block_length = 64
    total_blocks = RESIDUE_COUNT // block_length
    left_residue_blocks = alignment_left.reshape(total_blocks, block_length, CHANNEL_WIDTH, ALIGNMENT_ROWS)
    pair_blocks = pair_features.reshape(total_blocks, block_length, RESIDUE_COUNT, CZ)

    def one_block(inputs):
        left_residue_block, pair_block = inputs
        channel_products = lax.dot_general(left_residue_block, alignment_right, (((2,), (0,)), ((), ())), preferred_element_type=jnp.float32)
        outer_product_average = (channel_products / ALIGNMENT_ROWS).astype(jnp.bfloat16)
        outer_product_average = outer_product_average.reshape(block_length, CHANNEL_WIDTH, RESIDUE_COUNT, CHANNEL_WIDTH).transpose(0, 2, 1, 3).reshape(block_length * RESIDUE_COUNT, CHANNEL_WIDTH * CHANNEL_WIDTH)
        update = jnp.dot(outer_product_average, output_weight, preferred_element_type=jnp.float32) + output_bias
        fresh = (pair_block.astype(jnp.float32).reshape(block_length * RESIDUE_COUNT, CZ) + update).astype(jnp.bfloat16)
        projected = project(fresh, norm_scale_gain, projection_weight, gate_offset_bias)
        return (fresh.reshape(block_length, RESIDUE_COUNT, CZ), projected.reshape(block_length, RESIDUE_COUNT, PROJ))
    new_blocks, proj_blocks = lax.map(one_block, (left_residue_blocks, pair_blocks))
    new_pair = new_blocks.reshape(RESIDUE_COUNT, RESIDUE_COUNT, CZ)
    projections = jnp.transpose(proj_blocks.reshape(RESIDUE_COUNT, RESIDUE_COUNT, PROJ), (1, 2, 0))
    return (new_pair, projections)
```

```python
import functools

import jax
import jax.numpy as jnp
from jax import lax
from jax.experimental import pallas as pl
from jax.experimental.pallas import tpu as pltpu
from jax.sharding import PartitionSpec as P

CHANNEL_WIDTH = 32
CORES = 2
STEP = 16
VMEM_LIMIT = 50 * 1024 * 1024

norm_eps = 1e-05

NT = (((1,), (1,)), ((), ()))


def update_kernel(
    parts,
    part,
    where_ref,
    left_ref,
    *refs,
):
    rights = refs[:parts]
    pair_ref, weight_ref, bias_ref, gain_ref = refs[parts : parts + 4]
    new_ref, normed_ref, right_all, right_turned, outer, rows, sems = refs[-7:]
    tile_rows = pair_ref.shape[0]
    share = rights[0].shape[0]
    depth = share * parts
    width = STEP * CHANNEL_WIDTH
    mine = where_ref[0]
    copies = []
    for d in range(parts):
        source = rights[d].at[:, pl.ds(part * width, width)]
        place = pl.multiple_of((mine ^ d) * share, share)
        copy = pltpu.make_async_copy(source, right_all.at[pl.ds(place, share), :], sems.at[d])
        copy.start()
        copies.append(copy)
    rows[...] = pair_ref[...].astype(jnp.float32).reshape(tile_rows * STEP, -1)
    for copy in copies:
        copy.wait()
    right_turned[...] = right_all[...].T
    for c1 in range(0, CHANNEL_WIDTH, 2):
        both = jnp.concatenate(
            [left_ref[:, c * depth : (c + 1) * depth] for c in (c1, c1 + 1)], axis=0
        )
        product = lax.dot_general(right_turned[...], both, NT, preferred_element_type=jnp.float32)
        outer[:, c1 * tile_rows : (c1 + 2) * tile_rows] = (product * (1.0 / depth)).astype(jnp.bfloat16)
    for j in range(0, STEP, 2):
        columns = [
            jnp.concatenate(
                [
                    outer[
                        jj * CHANNEL_WIDTH : (jj + 1) * CHANNEL_WIDTH,
                        c1 * tile_rows : (c1 + 1) * tile_rows,
                    ]
                    for c1 in range(CHANNEL_WIDTH)
                ],
                axis=0,
            )
            for jj in (j, j + 1)
        ]
        update = jnp.dot(
            weight_ref[...], jnp.concatenate(columns, axis=1), preferred_element_type=jnp.float32
        )
        for jj in (j, j + 1):
            mine_update = update[:, (jj - j) * tile_rows : (jj - j + 1) * tile_rows] + bias_ref[...]
            place = pl.ds(jj, tile_rows, stride=STEP)
            fresh = rows[place, :].T + mine_update
            widened = fresh.astype(jnp.bfloat16).astype(jnp.float32)
            rows[place, :] = widened.T
            centred = widened - jnp.mean(widened, axis=0, keepdims=True)
            variance = jnp.mean(centred * centred, axis=0, keepdims=True)
            normed_ref[jj] = (centred * lax.rsqrt(variance + norm_eps) * gain_ref[...]).astype(jnp.bfloat16)
    new_ref[...] = rows[...].reshape(tile_rows, STEP, -1).astype(jnp.bfloat16)


def update_call(where, left, rights, pair, weight, bias, gain, earlier, part):
    tile_rows, tile_cols, channels = pair.shape
    parts = len(rights)
    depth = rights[0].shape[0] * parts
    width = STEP * CHANNEL_WIDTH
    whole = pl.BlockSpec(memory_space=pltpu.VMEM)
    far = pl.BlockSpec(memory_space=pl.ANY)
    block = pl.BlockSpec((tile_rows, STEP, channels), lambda g: (0, part, 0))
    args = [where, left, *rights, pair, weight, bias, gain]
    specs = [
        pl.BlockSpec(memory_space=pltpu.SMEM),
        whole,
        *[far] * parts,
        block,
        whole,
        whole,
        whole,
    ]
    aliases = {}
    if earlier is not None:
        aliases = {len(args): 0}
        args.append(earlier)
        specs.append(far)
    flops = 2 * width * CHANNEL_WIDTH * tile_rows * depth + 2 * STEP * tile_rows * CHANNEL_WIDTH**2 * channels
    return pl.pallas_call(
        functools.partial(update_kernel, parts, part),
        grid=(1,),
        in_specs=specs,
        out_specs=(block, pl.BlockSpec((STEP, channels, tile_rows), lambda g: (0, 0, 0))),
        out_shape=(
            jax.ShapeDtypeStruct(pair.shape, jnp.bfloat16),
            jax.ShapeDtypeStruct((STEP, channels, tile_rows), jnp.bfloat16),
        ),
        scratch_shapes=[
            pltpu.VMEM((depth, width), jnp.bfloat16),
            pltpu.VMEM((width, depth), jnp.bfloat16),
            pltpu.VMEM((width, CHANNEL_WIDTH * tile_rows), jnp.bfloat16),
            pltpu.VMEM((tile_rows * STEP, channels), jnp.float32),
            pltpu.SemaphoreType.DMA((parts,)),
        ],
        input_output_aliases=aliases,
        compiler_params=pltpu.CompilerParams(vmem_limit_bytes=VMEM_LIMIT),
        cost_estimate=pl.CostEstimate(flops=flops, bytes_accessed=8 * 2**20, transcendentals=0),
        name="update",
    )(*args)


def project_kernel(line, parts, where_ref, weight_ref, offset_ref, gate_ref, *refs):
    tiles = refs[: 2 * line - 1]
    outs = refs[2 * line - 1 : 2 * line - 1 + CORES * parts]
    held, sems = refs[-2:]
    mine, place = where_ref[0], where_ref[1]
    group = weight_ref.shape[0] // CORES
    lanes = held.shape[-1]

    def fetch(d):
        distance = (mine ^ d) - place
        for index in range(2 * line - 1):
            @pl.when(distance == index - (line - 1))
            def _():
                pltpu.make_async_copy(tiles[index], held.at[d % 2], sems.at[d % 2]).start()

    fetch(0)
    for d in range(parts):
        if d + 1 < parts:
            fetch(d + 1)
        pltpu.make_async_copy(tiles[0], held.at[d % 2], sems.at[d % 2]).wait()
        for j in range(0, STEP, 2):
            both = jnp.concatenate([held[d % 2, j], held[d % 2, j + 1]], axis=1)
            raw = jnp.dot(weight_ref[...], both, preferred_element_type=jnp.float32)
            gated = 1.0 / (1.0 + jnp.exp(-(raw + offset_ref[...])))
            result = jnp.where(gate_ref[...] > 0.0, gated, raw).astype(jnp.bfloat16)
            for e in range(CORES):
                for jj in range(2):
                    outs[d * CORES + e][j + jj] = result[
                        e * group : (e + 1) * group, jj * lanes : (jj + 1) * lanes
                    ]


def project_call(where, weight, offset, gate, tiles, parts):
    line = (len(tiles) + 1) // 2
    channels, lanes = tiles[0].shape[1:]
    group = weight.shape[0] // CORES
    whole = pl.BlockSpec(memory_space=pltpu.VMEM)
    far = pl.BlockSpec(memory_space=pl.ANY)
    shape = jax.ShapeDtypeStruct((STEP, group, lanes), jnp.bfloat16)
    return pl.pallas_call(
        functools.partial(project_kernel, line, parts),
        in_specs=[pl.BlockSpec(memory_space=pltpu.SMEM), whole, whole, whole, *[far] * len(tiles)],
        out_specs=[whole] * (CORES * parts),
        out_shape=[shape] * (CORES * parts),
        scratch_shapes=[
            pltpu.VMEM((2, STEP, channels, lanes), jnp.bfloat16),
            pltpu.SemaphoreType.DMA((2,)),
        ],
        compiler_params=pltpu.CompilerParams(vmem_limit_bytes=VMEM_LIMIT),
        cost_estimate=pl.CostEstimate(
            flops=2 * parts * STEP * channels * lanes * weight.shape[0],
            bytes_accessed=4 * 2**20,
            transcendentals=0,
        ),
        name="project",
    )(where, weight, offset, gate, *tiles)


def place_kernel(parts, part, tile_cols, where_ref, *refs):
    pieces = refs[: CORES * parts]
    out_ref, sems = refs[-2:]
    mine, core = where_ref[0], where_ref[2]
    step, group, lanes = pieces[0].shape
    copies = []
    for d in range(parts):
        for e in range(CORES):
            row = pl.multiple_of((core ^ e) * tile_cols + part * STEP, STEP)
            column = pl.multiple_of((mine ^ d) * lanes, lanes)
            copy = pltpu.make_async_copy(
                pieces[d * CORES + e],
                out_ref.at[pl.ds(row, step), :, pl.ds(column, lanes)],
                sems.at[d * CORES + e],
            )
            copy.start()
            copies.append(copy)
    for copy in copies:
        copy.wait()


def place_call(where, pieces, earlier, part, parts, tile_cols):
    step, group, lanes = pieces[0].shape
    far = pl.BlockSpec(memory_space=pl.ANY)
    args = [where, *pieces]
    aliases = {}
    if earlier is not None:
        aliases = {len(args): 0}
        args.append(earlier)
    return pl.pallas_call(
        functools.partial(place_kernel, parts, part, tile_cols),
        in_specs=[pl.BlockSpec(memory_space=pltpu.SMEM), *[far] * (len(args) - 1)],
        out_specs=far,
        out_shape=jax.ShapeDtypeStruct((CORES * tile_cols, group, parts * lanes), jnp.bfloat16),
        scratch_shapes=[pltpu.SemaphoreType.DMA((CORES * parts,))],
        input_output_aliases=aliases,
        cost_estimate=pl.CostEstimate(flops=0, bytes_accessed=4 * 2**20, transcendentals=0),
        name="place",
    )(*args)


def shards(
    alignment_left,
    alignment_right,
    pair_features,
    output_weight,
    output_bias,
    norm_scale_gain,
    projection_weight,
    gate_offset_bias,
):
    parts, cols = lax.axis_size("row"), lax.axis_size("col")
    line = cols // CORES
    assert line == parts
    tile_rows, tile_cols, channels = pair_features.shape
    row, col = lax.axis_index("row"), lax.axis_index("col")
    where = jnp.stack([row, col // CORES, col % CORES]).astype(jnp.int32)

    rights = [alignment_right]
    for d in range(1, parts):
        rights.append(lax.ppermute(alignment_right, "row", [(a, a ^ d) for a in range(parts)]))
    left = lax.all_gather(alignment_left, "col", axis=0, tiled=True)

    weight = output_weight.T
    bias = output_bias.reshape(channels, 1)
    gain = norm_scale_gain.reshape(channels, 1)

    total = projection_weight.shape[1]
    group = total // cols
    gate_start = total - gate_offset_bias.shape[0]
    turned = projection_weight.T
    offsets = jnp.concatenate([jnp.zeros((gate_start,), jnp.float32), gate_offset_bias]).reshape(total, 1)
    gates = (jnp.arange(total) >= gate_start).astype(jnp.float32).reshape(total, 1)

    def chosen(array):
        return jnp.concatenate(
            [lax.dynamic_slice_in_dim(array, (col ^ e) * group, group, 0) for e in range(CORES)], axis=0
        )

    my_weight, my_offsets, my_gates = chosen(turned), chosen(offsets), chosen(gates)

    new_pair, result = None, None
    for part in range(tile_cols // STEP):
        new_pair, normed = update_call(
            where, left, rights, pair_features, weight, bias, gain, new_pair, part
        )
        tiles = {0: normed}
        for s in range(1, line):
            up = [(z * CORES + k, (z + 1) * CORES + k) for z in range(s - 1, line - 1) for k in range(CORES)]
            down = [(cols - 1 - a, cols - 1 - b) for a, b in up]
            tiles[-s] = lax.ppermute(tiles[-(s - 1)], "col", up)
            tiles[s] = lax.ppermute(tiles[s - 1], "col", down)
        pieces = project_call(
            where,
            my_weight,
            my_offsets,
            my_gates,
            [tiles[o] for o in range(-(line - 1), line)],
            parts,
        )
        moved = []
        for d in range(parts):
            for e in range(CORES):
                piece = pieces[d * CORES + e]
                if d or e:
                    pairs = [
                        (a * cols + c, (a ^ d) * cols + (c ^ e)) for a in range(parts) for c in range(cols)
                    ]
                    piece = lax.ppermute(piece, ("row", "col"), pairs)
                moved.append(piece)
        result = place_call(where, moved, result, part, parts, tile_cols)
    return (new_pair, result)


def solution(mesh):
    placed = (
        P(("row", "col"), None),
        P("row", "col"),
        P("row", "col", None),
        P(),
        P(),
        P(),
        P(),
        P(),
    )
    return jax.shard_map(
        shards,
        mesh=mesh,
        in_specs=placed,
        out_specs=(P("row", "col", None), P("row", "col", None)),
        check_vma=False,
    )
```

```python
import functools

import jax
import jax.numpy as jnp
from jax import lax
from jax.experimental import pallas as pl
from jax.experimental.pallas import tpu as pltpu
from jax.sharding import PartitionSpec as P

CHANNEL_WIDTH = 32
CORES = 2
STEP = 16
VMEM_LIMIT = 50 * 1024 * 1024

norm_eps = 1e-05

NT = (((1,), (1,)), ((), ()))


def update_kernel(
    parts,
    part,
    where_ref,
    left_ref,
    *refs,
):
    rights = refs[:parts]
    pair_ref, weight_ref, bias_ref, gain_ref = refs[parts : parts + 4]
    new_ref, normed_ref, right_all, right_turned, outer, rows, sems = refs[-7:]
    tile_rows = pair_ref.shape[0]
    share = rights[0].shape[0]
    depth = share * parts
    width = STEP * CHANNEL_WIDTH
    mine = where_ref[0]
    copies = []
    for d in range(parts):
        source = rights[d].at[:, pl.ds(part * width, width)]
        place = pl.multiple_of((mine ^ d) * share, share)
        copy = pltpu.make_async_copy(source, right_all.at[pl.ds(place, share), :], sems.at[d])
        copy.start()
        copies.append(copy)
    rows[...] = pair_ref[...].astype(jnp.float32).reshape(tile_rows * STEP, -1)
    for copy in copies:
        copy.wait()
    right_turned[...] = right_all[...].T
    for c1 in range(0, CHANNEL_WIDTH, 2):
        both = jnp.concatenate(
            [left_ref[:, c * depth : (c + 1) * depth] for c in (c1, c1 + 1)], axis=0
        )
        product = lax.dot_general(right_turned[...], both, NT, preferred_element_type=jnp.float32)
        outer[:, c1 * tile_rows : (c1 + 2) * tile_rows] = (product * (1.0 / depth)).astype(jnp.bfloat16)
    for j in range(0, STEP, 2):
        columns = [
            jnp.concatenate(
                [
                    outer[
                        jj * CHANNEL_WIDTH : (jj + 1) * CHANNEL_WIDTH,
                        c1 * tile_rows : (c1 + 1) * tile_rows,
                    ]
                    for c1 in range(CHANNEL_WIDTH)
                ],
                axis=0,
            )
            for jj in (j, j + 1)
        ]
        update = jnp.dot(
            weight_ref[...], jnp.concatenate(columns, axis=1), preferred_element_type=jnp.float32
        )
        for jj in (j, j + 1):
            mine_update = update[:, (jj - j) * tile_rows : (jj - j + 1) * tile_rows] + bias_ref[...]
            place = pl.ds(jj, tile_rows, stride=STEP)
            fresh = rows[place, :].T + mine_update
            widened = fresh.astype(jnp.bfloat16).astype(jnp.float32)
            rows[place, :] = widened.T
            centred = widened - jnp.mean(widened, axis=0, keepdims=True)
            variance = jnp.mean(centred * centred, axis=0, keepdims=True)
            normed_ref[jj] = (centred * lax.rsqrt(variance + norm_eps) * gain_ref[...]).astype(jnp.bfloat16)
    new_ref[...] = rows[...].reshape(tile_rows, STEP, -1).astype(jnp.bfloat16)


def update_call(where, left, rights, pair, weight, bias, gain, earlier, part):
    tile_rows, tile_cols, channels = pair.shape
    parts = len(rights)
    depth = rights[0].shape[0] * parts
    width = STEP * CHANNEL_WIDTH
    whole = pl.BlockSpec(memory_space=pltpu.VMEM)
    far = pl.BlockSpec(memory_space=pl.ANY)
    block = pl.BlockSpec((tile_rows, STEP, channels), lambda g: (0, part, 0))
    args = [where, left, *rights, pair, weight, bias, gain]
    specs = [
        pl.BlockSpec(memory_space=pltpu.SMEM),
        whole,
        *[far] * parts,
        block,
        whole,
        whole,
        whole,
    ]
    aliases = {}
    if earlier is not None:
        aliases = {len(args): 0}
        args.append(earlier)
        specs.append(far)
    flops = 2 * width * CHANNEL_WIDTH * tile_rows * depth + 2 * STEP * tile_rows * CHANNEL_WIDTH**2 * channels
    return pl.pallas_call(
        functools.partial(update_kernel, parts, part),
        grid=(1,),
        in_specs=specs,
        out_specs=(block, pl.BlockSpec((STEP, channels, tile_rows), lambda g: (0, 0, 0))),
        out_shape=(
            jax.ShapeDtypeStruct(pair.shape, jnp.bfloat16),
            jax.ShapeDtypeStruct((STEP, channels, tile_rows), jnp.bfloat16),
        ),
        scratch_shapes=[
            pltpu.VMEM((depth, width), jnp.bfloat16),
            pltpu.VMEM((width, depth), jnp.bfloat16),
            pltpu.VMEM((width, CHANNEL_WIDTH * tile_rows), jnp.bfloat16),
            pltpu.VMEM((tile_rows * STEP, channels), jnp.float32),
            pltpu.SemaphoreType.DMA((parts,)),
        ],
        input_output_aliases=aliases,
        compiler_params=pltpu.CompilerParams(vmem_limit_bytes=VMEM_LIMIT),
        cost_estimate=pl.CostEstimate(flops=flops, bytes_accessed=8 * 2**20, transcendentals=0),
        name="update",
    )(*args)


def project_kernel(line, parts, where_ref, weight_ref, offset_ref, gate_ref, *refs):
    tiles = refs[: 2 * line - 1]
    outs = refs[2 * line - 1 : 2 * line - 1 + CORES * parts]
    held, sems = refs[-2:]
    mine, place = where_ref[0], where_ref[1]
    group = weight_ref.shape[0] // CORES
    lanes = held.shape[-1]

    def fetch(d):
        distance = (mine ^ d) - place
        for index in range(2 * line - 1):
            @pl.when(distance == index - (line - 1))
            def _():
                pltpu.make_async_copy(tiles[index], held.at[d % 2], sems.at[d % 2]).start()

    fetch(0)
    for d in range(parts):
        if d + 1 < parts:
            fetch(d + 1)
        pltpu.make_async_copy(tiles[0], held.at[d % 2], sems.at[d % 2]).wait()
        for j in range(0, STEP, 2):
            both = jnp.concatenate([held[d % 2, j], held[d % 2, j + 1]], axis=1)
            raw = jnp.dot(weight_ref[...], both, preferred_element_type=jnp.float32)
            gated = 1.0 / (1.0 + jnp.exp(-(raw + offset_ref[...])))
            result = jnp.where(gate_ref[...] > 0.0, gated, raw).astype(jnp.bfloat16)
            for e in range(CORES):
                for jj in range(2):
                    outs[d * CORES + e][j + jj] = result[
                        e * group : (e + 1) * group, jj * lanes : (jj + 1) * lanes
                    ]


def project_call(where, weight, offset, gate, tiles, parts):
    line = (len(tiles) + 1) // 2
    channels, lanes = tiles[0].shape[1:]
    group = weight.shape[0] // CORES
    whole = pl.BlockSpec(memory_space=pltpu.VMEM)
    far = pl.BlockSpec(memory_space=pl.ANY)
    shape = jax.ShapeDtypeStruct((STEP, group, lanes), jnp.bfloat16)
    return pl.pallas_call(
        functools.partial(project_kernel, line, parts),
        in_specs=[pl.BlockSpec(memory_space=pltpu.SMEM), whole, whole, whole, *[far] * len(tiles)],
        out_specs=[whole] * (CORES * parts),
        out_shape=[shape] * (CORES * parts),
        scratch_shapes=[
            pltpu.VMEM((2, STEP, channels, lanes), jnp.bfloat16),
            pltpu.SemaphoreType.DMA((2,)),
        ],
        compiler_params=pltpu.CompilerParams(vmem_limit_bytes=VMEM_LIMIT),
        cost_estimate=pl.CostEstimate(
            flops=2 * parts * STEP * channels * lanes * weight.shape[0],
            bytes_accessed=4 * 2**20,
            transcendentals=0,
        ),
        name="project",
    )(where, weight, offset, gate, *tiles)


def place_kernel(parts, part, tile_cols, where_ref, *refs):
    pieces = refs[: CORES * parts]
    out_ref, rows, sems = refs[-3:]
    mine, core = where_ref[0], where_ref[2]
    step, group, lanes = pieces[0].shape
    copies = []
    for e in range(CORES):
        for d in range(parts):
            column = pl.multiple_of((mine ^ d) * lanes, lanes)
            rows[e, :, :, pl.ds(column, lanes)] = pieces[d * CORES + e][...]
        row = pl.multiple_of((core ^ e) * tile_cols + part * STEP, STEP)
        copy = pltpu.make_async_copy(rows.at[e], out_ref.at[pl.ds(row, step)], sems.at[e])
        copy.start()
        copies.append(copy)
    for copy in copies:
        copy.wait()


def place_call(where, pieces, earlier, part, parts, tile_cols):
    step, group, lanes = pieces[0].shape
    far = pl.BlockSpec(memory_space=pl.ANY)
    whole = pl.BlockSpec(memory_space=pltpu.VMEM)
    args = [where, *pieces]
    specs = [pl.BlockSpec(memory_space=pltpu.SMEM), *[whole] * len(pieces)]
    aliases = {}
    if earlier is not None:
        aliases = {len(args): 0}
        args.append(earlier)
        specs.append(far)
    return pl.pallas_call(
        functools.partial(place_kernel, parts, part, tile_cols),
        in_specs=specs,
        out_specs=far,
        out_shape=jax.ShapeDtypeStruct((CORES * tile_cols, group, parts * lanes), jnp.bfloat16),
        scratch_shapes=[
            pltpu.VMEM((CORES, step, group, parts * lanes), jnp.bfloat16),
            pltpu.SemaphoreType.DMA((CORES,)),
        ],
        input_output_aliases=aliases,
        compiler_params=pltpu.CompilerParams(vmem_limit_bytes=VMEM_LIMIT),
        cost_estimate=pl.CostEstimate(flops=0, bytes_accessed=8 * 2**20, transcendentals=0),
        name="place",
    )(*args)


def shards(
    alignment_left,
    alignment_right,
    pair_features,
    output_weight,
    output_bias,
    norm_scale_gain,
    projection_weight,
    gate_offset_bias,
):
    parts, cols = lax.axis_size("row"), lax.axis_size("col")
    line = cols // CORES
    assert line == parts
    tile_rows, tile_cols, channels = pair_features.shape
    row, col = lax.axis_index("row"), lax.axis_index("col")
    where = jnp.stack([row, col // CORES, col % CORES]).astype(jnp.int32)

    rights = [alignment_right]
    for d in range(1, parts):
        rights.append(lax.ppermute(alignment_right, "row", [(a, a ^ d) for a in range(parts)]))
    left = lax.all_gather(alignment_left, "col", axis=0, tiled=True)

    weight = output_weight.T
    bias = output_bias.reshape(channels, 1)
    gain = norm_scale_gain.reshape(channels, 1)

    total = projection_weight.shape[1]
    group = total // cols
    gate_start = total - gate_offset_bias.shape[0]
    turned = projection_weight.T
    offsets = jnp.concatenate([jnp.zeros((gate_start,), jnp.float32), gate_offset_bias]).reshape(total, 1)
    gates = (jnp.arange(total) >= gate_start).astype(jnp.float32).reshape(total, 1)

    def chosen(array):
        return jnp.concatenate(
            [lax.dynamic_slice_in_dim(array, (col ^ e) * group, group, 0) for e in range(CORES)], axis=0
        )

    my_weight, my_offsets, my_gates = chosen(turned), chosen(offsets), chosen(gates)

    count = tile_cols // STEP
    state = {"new_pair": None, "result": None}
    tiles = [{} for _ in range(count)]
    moved = [None] * count

    def after(value, *others):
        return lax.optimization_barrier((value, others))[0]

    def update(part, *others):
        state["new_pair"], tiles[part][0] = update_call(
            after(where, *others), left, rights, pair_features, weight, bias, gain, state["new_pair"], part
        )

    def shift(part, s, *others):
        up = [(z * CORES + k, (z + 1) * CORES + k) for z in range(s - 1, line - 1) for k in range(CORES)]
        down = [(cols - 1 - a, cols - 1 - b) for a, b in up]
        here = tiles[part]
        here[-s] = lax.ppermute(after(here[-(s - 1)], *others), "col", up)
        here[s] = lax.ppermute(after(here[s - 1], *others), "col", down)

    def send(part, *others):
        here = tiles[part]
        pieces = project_call(
            after(where, *others),
            my_weight,
            my_offsets,
            my_gates,
            [here[o] for o in range(-(line - 1), line)],
            parts,
        )
        moved[part] = []
        for d in range(parts):
            for e in range(CORES):
                piece = pieces[d * CORES + e]
                if d or e:
                    pairs = [
                        (a * cols + c, (a ^ d) * cols + (c ^ e)) for a in range(parts) for c in range(cols)
                    ]
                    piece = lax.ppermute(piece, ("row", "col"), pairs)
                moved[part].append(piece)

    def place(part):
        state["result"] = place_call(where, moved[part], state["result"], part, parts, tile_cols)

    update(0)
    for part in range(count):
        for s in range(1, line):
            others = moved[part - 1] if part and s == line - 1 else []
            shift(part, s, *others)
            if s == 1 and part + 1 < count:
                update(part + 1, tiles[part][-1])
        send(part)
    for part in range(count):
        place(part)
    return (state["new_pair"], state["result"])


def solution(mesh):
    placed = (
        P(("row", "col"), None),
        P("row", "col"),
        P("row", "col", None),
        P(),
        P(),
        P(),
        P(),
        P(),
    )
    return jax.shard_map(
        shards,
        mesh=mesh,
        in_specs=placed,
        out_specs=(P("row", "col", None), P("row", "col", None)),
        check_vma=False,
    )
```

```python
import functools

import jax
import jax.numpy as jnp
from jax import lax
from jax.experimental import pallas as pl
from jax.experimental.pallas import tpu as pltpu
from jax.sharding import PartitionSpec as P

CHANNEL_WIDTH = 32
CORES = 2
STEP = 16
VMEM_LIMIT = 50 * 1024 * 1024

norm_eps = 1e-05

NT = (((1,), (1,)), ((), ()))


def update_kernel(
    parts,
    part,
    where_ref,
    left_ref,
    *refs,
):
    rights = refs[:parts]
    pair_ref, weight_ref, bias_ref, gain_ref = refs[parts : parts + 4]
    new_ref, normed_ref, right_all, right_turned, outer, rows, sems = refs[-7:]
    tile_rows = pair_ref.shape[0]
    share = rights[0].shape[0]
    depth = share * parts
    width = STEP * CHANNEL_WIDTH
    mine = where_ref[0]
    copies = []
    for d in range(parts):
        source = rights[d].at[:, pl.ds(part * width, width)]
        place = pl.multiple_of((mine ^ d) * share, share)
        copy = pltpu.make_async_copy(source, right_all.at[pl.ds(place, share), :], sems.at[d])
        copy.start()
        copies.append(copy)
    rows[...] = pair_ref[...].astype(jnp.float32).reshape(tile_rows * STEP, -1)
    for copy in copies:
        copy.wait()
    right_turned[...] = right_all[...].T
    for c1 in range(0, CHANNEL_WIDTH, 2):
        both = jnp.concatenate(
            [left_ref[:, c * depth : (c + 1) * depth] for c in (c1, c1 + 1)], axis=0
        )
        product = lax.dot_general(right_turned[...], both, NT, preferred_element_type=jnp.float32)
        outer[:, c1 * tile_rows : (c1 + 2) * tile_rows] = (product * (1.0 / depth)).astype(jnp.bfloat16)
    for j in range(0, STEP, 2):
        columns = [
            jnp.concatenate(
                [
                    outer[
                        jj * CHANNEL_WIDTH : (jj + 1) * CHANNEL_WIDTH,
                        c1 * tile_rows : (c1 + 1) * tile_rows,
                    ]
                    for c1 in range(CHANNEL_WIDTH)
                ],
                axis=0,
            )
            for jj in (j, j + 1)
        ]
        update = jnp.dot(
            weight_ref[...], jnp.concatenate(columns, axis=1), preferred_element_type=jnp.float32
        )
        for jj in (j, j + 1):
            mine_update = update[:, (jj - j) * tile_rows : (jj - j + 1) * tile_rows] + bias_ref[...]
            place = pl.ds(jj, tile_rows, stride=STEP)
            fresh = rows[place, :].T + mine_update
            widened = fresh.astype(jnp.bfloat16).astype(jnp.float32)
            rows[place, :] = widened.T
            centred = widened - jnp.mean(widened, axis=0, keepdims=True)
            variance = jnp.mean(centred * centred, axis=0, keepdims=True)
            normed_ref[jj] = (centred * lax.rsqrt(variance + norm_eps) * gain_ref[...]).astype(jnp.bfloat16)
    new_ref[...] = rows[...].reshape(tile_rows, STEP, -1).astype(jnp.bfloat16)


def update_call(where, left, rights, pair, weight, bias, gain, earlier, part):
    tile_rows, tile_cols, channels = pair.shape
    parts = len(rights)
    depth = rights[0].shape[0] * parts
    width = STEP * CHANNEL_WIDTH
    whole = pl.BlockSpec(memory_space=pltpu.VMEM)
    far = pl.BlockSpec(memory_space=pl.ANY)
    block = pl.BlockSpec((tile_rows, STEP, channels), lambda g: (0, part, 0))
    args = [where, left, *rights, pair, weight, bias, gain]
    specs = [
        pl.BlockSpec(memory_space=pltpu.SMEM),
        whole,
        *[far] * parts,
        block,
        whole,
        whole,
        whole,
    ]
    aliases = {}
    if earlier is not None:
        aliases = {len(args): 0}
        args.append(earlier)
        specs.append(far)
    flops = 2 * width * CHANNEL_WIDTH * tile_rows * depth + 2 * STEP * tile_rows * CHANNEL_WIDTH**2 * channels
    return pl.pallas_call(
        functools.partial(update_kernel, parts, part),
        grid=(1,),
        in_specs=specs,
        out_specs=(block, pl.BlockSpec((STEP, channels, tile_rows), lambda g: (0, 0, 0))),
        out_shape=(
            jax.ShapeDtypeStruct(pair.shape, jnp.bfloat16),
            jax.ShapeDtypeStruct((STEP, channels, tile_rows), jnp.bfloat16),
        ),
        scratch_shapes=[
            pltpu.VMEM((depth, width), jnp.bfloat16),
            pltpu.VMEM((width, depth), jnp.bfloat16),
            pltpu.VMEM((width, CHANNEL_WIDTH * tile_rows), jnp.bfloat16),
            pltpu.VMEM((tile_rows * STEP, channels), jnp.float32),
            pltpu.SemaphoreType.DMA((parts,)),
        ],
        input_output_aliases=aliases,
        compiler_params=pltpu.CompilerParams(vmem_limit_bytes=VMEM_LIMIT),
        cost_estimate=pl.CostEstimate(flops=flops, bytes_accessed=8 * 2**20, transcendentals=0),
        name="update",
    )(*args)


def project_kernel(line, parts, where_ref, weight_ref, offset_ref, gate_ref, *refs):
    tiles = refs[: 2 * line - 1]
    outs = refs[2 * line - 1 : 2 * line - 1 + parts]
    held, sems = refs[-2:]
    mine, place, core = where_ref[0], where_ref[1], where_ref[2]
    group = weight_ref.shape[0] // CORES
    lanes = held.shape[-1]

    def fetch(d):
        distance = ((mine ^ d) - place) * (1 - 2 * core)
        for index in range(2 * line - 1):
            @pl.when(distance == index - (line - 1))
            def _():
                pltpu.make_async_copy(tiles[index], held.at[d % 2], sems.at[d % 2]).start()

    fetch(0)
    for d in range(parts):
        if d + 1 < parts:
            fetch(d + 1)
        pltpu.make_async_copy(tiles[0], held.at[d % 2], sems.at[d % 2]).wait()
        for j in range(0, STEP, 2):
            both = jnp.concatenate([held[d % 2, j], held[d % 2, j + 1]], axis=1)
            raw = jnp.dot(weight_ref[...], both, preferred_element_type=jnp.float32)
            gated = 1.0 / (1.0 + jnp.exp(-(raw + offset_ref[...])))
            result = jnp.where(gate_ref[...] > 0.0, gated, raw).astype(jnp.bfloat16)
            for e in range(CORES):
                for jj in range(2):
                    outs[d][e, j + jj] = result[e * group : (e + 1) * group, jj * lanes : (jj + 1) * lanes]


def project_call(where, weight, offset, gate, tiles, parts):
    line = (len(tiles) + 1) // 2
    channels, lanes = tiles[0].shape[1:]
    group = weight.shape[0] // CORES
    whole = pl.BlockSpec(memory_space=pltpu.VMEM)
    far = pl.BlockSpec(memory_space=pl.ANY)
    shape = jax.ShapeDtypeStruct((CORES, STEP, group, lanes), jnp.bfloat16)
    return pl.pallas_call(
        functools.partial(project_kernel, line, parts),
        in_specs=[pl.BlockSpec(memory_space=pltpu.SMEM), whole, whole, whole, *[far] * len(tiles)],
        out_specs=[whole] * parts,
        out_shape=[shape] * parts,
        scratch_shapes=[
            pltpu.VMEM((2, STEP, channels, lanes), jnp.bfloat16),
            pltpu.SemaphoreType.DMA((2,)),
        ],
        compiler_params=pltpu.CompilerParams(vmem_limit_bytes=VMEM_LIMIT),
        cost_estimate=pl.CostEstimate(
            flops=2 * parts * STEP * channels * lanes * weight.shape[0],
            bytes_accessed=4 * 2**20,
            transcendentals=0,
        ),
        name="project",
    )(where, weight, offset, gate, *tiles)


def place_kernel(parts, part, tile_cols, where_ref, *refs):
    pieces = refs[:parts]
    out_ref, other_ref, rows, sem = refs[-4:]
    mine, core = where_ref[0], where_ref[2]
    step, group, lanes = pieces[0].shape[1:]
    for e, target in enumerate((rows, other_ref)):
        for d in range(parts):
            column = pl.multiple_of((mine ^ d) * lanes, lanes)
            target[:, :, pl.ds(column, lanes)] = pieces[d][e]
        if e == 0:
            row = pl.multiple_of(core * tile_cols + part * step, step)
            copy = pltpu.make_async_copy(rows, out_ref.at[pl.ds(row, step)], sem)
            copy.start()
    copy.wait()


def place_call(where, pieces, earlier, part, parts, tile_cols):
    step, group, lanes = pieces[0].shape[1:]
    far = pl.BlockSpec(memory_space=pl.ANY)
    whole = pl.BlockSpec(memory_space=pltpu.VMEM)
    args = [where, *pieces]
    specs = [pl.BlockSpec(memory_space=pltpu.SMEM), *[whole] * len(pieces)]
    aliases = {}
    if earlier is not None:
        aliases = {len(args): 0}
        args.append(earlier)
        specs.append(far)
    block = (step, group, parts * lanes)
    return pl.pallas_call(
        functools.partial(place_kernel, parts, part, tile_cols),
        in_specs=specs,
        out_specs=(far, whole),
        out_shape=(
            jax.ShapeDtypeStruct((CORES * tile_cols, *block[1:]), jnp.bfloat16),
            jax.ShapeDtypeStruct(block, jnp.bfloat16),
        ),
        scratch_shapes=[pltpu.VMEM(block, jnp.bfloat16), pltpu.SemaphoreType.DMA],
        input_output_aliases=aliases,
        compiler_params=pltpu.CompilerParams(vmem_limit_bytes=VMEM_LIMIT),
        cost_estimate=pl.CostEstimate(flops=0, bytes_accessed=6 * 2**20, transcendentals=0),
        name="place",
    )(*args)


def put_kernel(part, tile_cols, where_ref, rows_ref, earlier_ref, out_ref, sem):
    del earlier_ref
    row = pl.multiple_of((1 - where_ref[2]) * tile_cols + part * rows_ref.shape[0], rows_ref.shape[0])
    copy = pltpu.make_async_copy(rows_ref, out_ref.at[pl.ds(row, rows_ref.shape[0])], sem)
    copy.start()
    copy.wait()


def put_call(where, rows, earlier, part, tile_cols):
    far = pl.BlockSpec(memory_space=pl.ANY)
    return pl.pallas_call(
        functools.partial(put_kernel, part, tile_cols),
        in_specs=[pl.BlockSpec(memory_space=pltpu.SMEM), pl.BlockSpec(memory_space=pltpu.VMEM), far],
        out_specs=far,
        out_shape=jax.ShapeDtypeStruct(earlier.shape, earlier.dtype),
        scratch_shapes=[pltpu.SemaphoreType.DMA],
        input_output_aliases={2: 0},
        compiler_params=pltpu.CompilerParams(vmem_limit_bytes=VMEM_LIMIT),
        cost_estimate=pl.CostEstimate(flops=0, bytes_accessed=2 * 2**20, transcendentals=0),
        name="put",
    )(where, rows, earlier)


def shards(
    alignment_left,
    alignment_right,
    pair_features,
    output_weight,
    output_bias,
    norm_scale_gain,
    projection_weight,
    gate_offset_bias,
):
    parts, cols = lax.axis_size("row"), lax.axis_size("col")
    line = cols // CORES
    assert line == parts
    tile_rows, tile_cols, channels = pair_features.shape
    row, col = lax.axis_index("row"), lax.axis_index("col")
    where = jnp.stack([row, col // CORES, col % CORES]).astype(jnp.int32)

    rights = [alignment_right]
    for d in range(1, parts):
        rights.append(lax.ppermute(alignment_right, "row", [(a, a ^ d) for a in range(parts)]))
    left = lax.all_gather(alignment_left, "col", axis=0, tiled=True)

    weight = output_weight.T
    bias = output_bias.reshape(channels, 1)
    gain = norm_scale_gain.reshape(channels, 1)

    total = projection_weight.shape[1]
    group = total // cols
    gate_start = total - gate_offset_bias.shape[0]
    turned = projection_weight.T
    offsets = jnp.concatenate([jnp.zeros((gate_start,), jnp.float32), gate_offset_bias]).reshape(total, 1)
    gates = (jnp.arange(total) >= gate_start).astype(jnp.float32).reshape(total, 1)

    def chosen(array):
        return jnp.concatenate(
            [lax.dynamic_slice_in_dim(array, (col ^ e) * group, group, 0) for e in range(CORES)], axis=0
        )

    my_weight, my_offsets, my_gates = chosen(turned), chosen(offsets), chosen(gates)

    count = tile_cols // STEP
    state = {"new_pair": None, "result": None}
    tiles = [{} for _ in range(count)]
    moved = [None] * count

    def after(value, *others):
        return lax.optimization_barrier((value, others))[0]

    def update(part, *others):
        state["new_pair"], tiles[part][0] = update_call(
            after(where, *others), left, rights, pair_features, weight, bias, gain, state["new_pair"], part
        )

    ring = [z * CORES for z in range(line)] + [z * CORES + 1 for z in reversed(range(line))]
    onward = [(ring[t], ring[(t + 1) % cols]) for t in range(cols)]
    back = [(b, a) for a, b in onward]

    def shift(part, s, *others):
        here = tiles[part]
        here[-s] = lax.ppermute(after(here[-(s - 1)], *others), "col", onward)
        here[s] = lax.ppermute(after(here[s - 1], *others), "col", back)

    def project(part, *others):
        here = tiles[part]
        moved[part] = list(
            project_call(
                after(where, *others),
                my_weight,
                my_offsets,
                my_gates,
                [here[o] for o in range(-(line - 1), line)],
                parts,
            )
        )

    def send(part, d):
        moved[part][d] = lax.ppermute(moved[part][d], "row", [(a, a ^ d) for a in range(parts)])

    def place(part):
        state["result"], other = place_call(where, moved[part], state["result"], part, parts, tile_cols)
        swapped[part] = lax.ppermute(other, "col", [(c, c ^ 1) for c in range(cols)])

    def put(part):
        state["result"] = put_call(where, swapped[part], state["result"], part, tile_cols)

    order = sorted(
        ((part, s) for part in range(count) for s in range(1, line)),
        key=lambda step: (step[0] + step[1], step[0]),
    )
    swapped = [None] * count
    done = []
    pending = []
    update(0)
    updated = 1
    for index, (part, s) in enumerate(order):
        others = list(done[index - 2]) if index >= 2 else []
        while updated <= part:
            update(updated)
            updated += 1
        if pending and index >= pending[0][0]:
            _, owner, d = pending.pop(0)
            others.append(moved[owner][d])
        if part == count - 1 and s == line - 1:
            for owner in range(count - 3):
                if swapped[owner] is not None:
                    others.append(swapped[owner])
        shift(part, s, *others)
        done.append((tiles[part][-s], tiles[part][s]))
        if updated < count and any(p == updated for p, _ in order[index + 2 : index + 4]):
            update(updated, *done[index - 1 if index else 0])
            updated += 1
        if s == line - 1 and part < count - 1:
            project(part)
            for d in range(1, parts):
                send(part, d)
                pending.append((index + 2 + d, part, d))
            place(part)
    project(count - 1, *[w for w in swapped[:-2] if w is not None])
    for d in range(1, parts):
        send(count - 1, d)
    for part in range(count - 1):
        put(part)
    place(count - 1)
    put(count - 1)
    return (state["new_pair"], state["result"])


def solution(mesh):
    placed = (
        P(("row", "col"), None),
        P("row", "col"),
        P("row", "col", None),
        P(),
        P(),
        P(),
        P(),
        P(),
    )
    return jax.shard_map(
        shards,
        mesh=mesh,
        in_specs=placed,
        out_specs=(P("row", "col", None), P("row", "col", None)),
        check_vma=False,
    )
```

```python
import functools

import jax
import jax.numpy as jnp
from jax import lax
from jax.experimental import pallas as pl
from jax.experimental.pallas import tpu as pltpu
from jax.sharding import PartitionSpec as P

CHANNEL_WIDTH = 32
CORES = 2
STEP = 16
VMEM_LIMIT = 50 * 1024 * 1024

norm_eps = 1e-05

NT = (((1,), (1,)), ((), ()))


def update_kernel(
    parts,
    part,
    where_ref,
    left_ref,
    *refs,
):
    rights = refs[:parts]
    pair_ref, weight_ref, bias_ref, gain_ref = refs[parts : parts + 4]
    new_ref, normed_ref, right_all, right_turned, outer, rows, sems = refs[-7:]
    tile_rows = pair_ref.shape[0]
    share = rights[0].shape[0]
    depth = share * parts
    width = STEP * CHANNEL_WIDTH
    mine = where_ref[0]
    copies = []
    for d in range(parts):
        source = rights[d].at[:, pl.ds(part * width, width)]
        place = pl.multiple_of((mine ^ d) * share, share)
        copy = pltpu.make_async_copy(source, right_all.at[pl.ds(place, share), :], sems.at[d])
        copy.start()
        copies.append(copy)
    rows[...] = pair_ref[...].astype(jnp.float32).reshape(tile_rows * STEP, -1)
    for copy in copies:
        copy.wait()
    right_turned[...] = right_all[...].T
    for c1 in range(0, CHANNEL_WIDTH, 2):
        both = jnp.concatenate(
            [left_ref[:, c * depth : (c + 1) * depth] for c in (c1, c1 + 1)], axis=0
        )
        product = lax.dot_general(right_turned[...], both, NT, preferred_element_type=jnp.float32)
        outer[:, c1 * tile_rows : (c1 + 2) * tile_rows] = (product * (1.0 / depth)).astype(jnp.bfloat16)
    for j in range(0, STEP, 2):
        columns = [
            jnp.concatenate(
                [
                    outer[
                        jj * CHANNEL_WIDTH : (jj + 1) * CHANNEL_WIDTH,
                        c1 * tile_rows : (c1 + 1) * tile_rows,
                    ]
                    for c1 in range(CHANNEL_WIDTH)
                ],
                axis=0,
            )
            for jj in (j, j + 1)
        ]
        update = jnp.dot(
            weight_ref[...], jnp.concatenate(columns, axis=1), preferred_element_type=jnp.float32
        )
        for jj in (j, j + 1):
            mine_update = update[:, (jj - j) * tile_rows : (jj - j + 1) * tile_rows] + bias_ref[...]
            place = pl.ds(jj, tile_rows, stride=STEP)
            fresh = rows[place, :].T + mine_update
            widened = fresh.astype(jnp.bfloat16).astype(jnp.float32)
            rows[place, :] = widened.T
            centred = widened - jnp.mean(widened, axis=0, keepdims=True)
            variance = jnp.mean(centred * centred, axis=0, keepdims=True)
            normed_ref[jj] = (centred * lax.rsqrt(variance + norm_eps) * gain_ref[...]).astype(jnp.bfloat16)
    new_ref[...] = rows[...].reshape(tile_rows, STEP, -1).astype(jnp.bfloat16)


def update_call(where, left, rights, pair, weight, bias, gain, earlier, part):
    tile_rows, tile_cols, channels = pair.shape
    parts = len(rights)
    depth = rights[0].shape[0] * parts
    width = STEP * CHANNEL_WIDTH
    whole = pl.BlockSpec(memory_space=pltpu.VMEM)
    far = pl.BlockSpec(memory_space=pl.ANY)
    block = pl.BlockSpec((tile_rows, STEP, channels), lambda g: (0, part, 0))
    args = [where, left, *rights, pair, weight, bias, gain]
    specs = [
        pl.BlockSpec(memory_space=pltpu.SMEM),
        whole,
        *[far] * parts,
        block,
        whole,
        whole,
        whole,
    ]
    aliases = {}
    if earlier is not None:
        aliases = {len(args): 0}
        args.append(earlier)
        specs.append(far)
    flops = 2 * width * CHANNEL_WIDTH * tile_rows * depth + 2 * STEP * tile_rows * CHANNEL_WIDTH**2 * channels
    return pl.pallas_call(
        functools.partial(update_kernel, parts, part),
        grid=(1,),
        in_specs=specs,
        out_specs=(block, pl.BlockSpec((STEP, channels, tile_rows), lambda g: (0, 0, 0))),
        out_shape=(
            jax.ShapeDtypeStruct(pair.shape, jnp.bfloat16),
            jax.ShapeDtypeStruct((STEP, channels, tile_rows), jnp.bfloat16),
        ),
        scratch_shapes=[
            pltpu.VMEM((depth, width), jnp.bfloat16),
            pltpu.VMEM((width, depth), jnp.bfloat16),
            pltpu.VMEM((width, CHANNEL_WIDTH * tile_rows), jnp.bfloat16),
            pltpu.VMEM((tile_rows * STEP, channels), jnp.float32),
            pltpu.SemaphoreType.DMA((parts,)),
        ],
        input_output_aliases=aliases,
        compiler_params=pltpu.CompilerParams(vmem_limit_bytes=VMEM_LIMIT),
        cost_estimate=pl.CostEstimate(flops=flops, bytes_accessed=8 * 2**20, transcendentals=0),
        name="update",
    )(*args)


def project_kernel(line, parts, where_ref, weight_ref, offset_ref, gate_ref, *refs):
    tiles = refs[: 2 * line - 1]
    outs = refs[2 * line - 1 : 2 * line - 1 + parts]
    held, sems = refs[-2:]
    mine, place, core = where_ref[0], where_ref[1], where_ref[2]
    group = weight_ref.shape[0] // CORES
    lanes = held.shape[-1]

    def fetch(d):
        distance = ((mine ^ d) - place) * (1 - 2 * core)
        for index in range(2 * line - 1):
            @pl.when(distance == index - (line - 1))
            def _():
                pltpu.make_async_copy(tiles[index], held.at[d % 2], sems.at[d % 2]).start()

    fetch(0)
    for d in range(parts):
        if d + 1 < parts:
            fetch(d + 1)
        pltpu.make_async_copy(tiles[0], held.at[d % 2], sems.at[d % 2]).wait()
        for j in range(0, STEP, 2):
            both = jnp.concatenate([held[d % 2, j], held[d % 2, j + 1]], axis=1)
            raw = jnp.dot(weight_ref[...], both, preferred_element_type=jnp.float32)
            gated = 1.0 / (1.0 + jnp.exp(-(raw + offset_ref[...])))
            result = jnp.where(gate_ref[...] > 0.0, gated, raw).astype(jnp.bfloat16)
            for e in range(CORES):
                for jj in range(2):
                    outs[d][e, j + jj] = result[e * group : (e + 1) * group, jj * lanes : (jj + 1) * lanes]


def project_call(where, weight, offset, gate, tiles, parts):
    line = (len(tiles) + 1) // 2
    channels, lanes = tiles[0].shape[1:]
    group = weight.shape[0] // CORES
    whole = pl.BlockSpec(memory_space=pltpu.VMEM)
    far = pl.BlockSpec(memory_space=pl.ANY)
    shape = jax.ShapeDtypeStruct((CORES, STEP, group, lanes), jnp.bfloat16)
    return pl.pallas_call(
        functools.partial(project_kernel, line, parts),
        in_specs=[pl.BlockSpec(memory_space=pltpu.SMEM), whole, whole, whole, *[far] * len(tiles)],
        out_specs=[whole] * parts,
        out_shape=[shape] * parts,
        scratch_shapes=[
            pltpu.VMEM((2, STEP, channels, lanes), jnp.bfloat16),
            pltpu.SemaphoreType.DMA((2,)),
        ],
        compiler_params=pltpu.CompilerParams(vmem_limit_bytes=VMEM_LIMIT),
        cost_estimate=pl.CostEstimate(
            flops=2 * parts * STEP * channels * lanes * weight.shape[0],
            bytes_accessed=4 * 2**20,
            transcendentals=0,
        ),
        name="project",
    )(where, weight, offset, gate, *tiles)


def place_kernel(parts, part, tile_cols, where_ref, *refs):
    pieces = refs[:parts]
    out_ref, other_ref, rows, sem = refs[-4:]
    mine, core = where_ref[0], where_ref[2]
    step, group, lanes = pieces[0].shape[1:]
    for e, target in enumerate((rows, other_ref)):
        for d in range(parts):
            column = pl.multiple_of((mine ^ d) * lanes, lanes)
            target[:, :, pl.ds(column, lanes)] = pieces[d][e]
        if e == 0:
            row = pl.multiple_of(core * tile_cols + part * step, step)
            copy = pltpu.make_async_copy(rows, out_ref.at[pl.ds(row, step)], sem)
            copy.start()
    copy.wait()


def place_call(where, pieces, earlier, part, parts, tile_cols):
    step, group, lanes = pieces[0].shape[1:]
    far = pl.BlockSpec(memory_space=pl.ANY)
    whole = pl.BlockSpec(memory_space=pltpu.VMEM)
    args = [where, *pieces]
    specs = [pl.BlockSpec(memory_space=pltpu.SMEM), *[whole] * len(pieces)]
    aliases = {}
    if earlier is not None:
        aliases = {len(args): 0}
        args.append(earlier)
        specs.append(far)
    block = (step, group, parts * lanes)
    return pl.pallas_call(
        functools.partial(place_kernel, parts, part, tile_cols),
        in_specs=specs,
        out_specs=(far, whole),
        out_shape=(
            jax.ShapeDtypeStruct((CORES * tile_cols, *block[1:]), jnp.bfloat16),
            jax.ShapeDtypeStruct(block, jnp.bfloat16),
        ),
        scratch_shapes=[pltpu.VMEM(block, jnp.bfloat16), pltpu.SemaphoreType.DMA],
        input_output_aliases=aliases,
        compiler_params=pltpu.CompilerParams(vmem_limit_bytes=VMEM_LIMIT),
        cost_estimate=pl.CostEstimate(flops=0, bytes_accessed=6 * 2**20, transcendentals=0),
        name="place",
    )(*args)


def put_kernel(part, tile_cols, where_ref, rows_ref, earlier_ref, out_ref, sem):
    del earlier_ref
    row = pl.multiple_of((1 - where_ref[2]) * tile_cols + part * rows_ref.shape[0], rows_ref.shape[0])
    copy = pltpu.make_async_copy(rows_ref, out_ref.at[pl.ds(row, rows_ref.shape[0])], sem)
    copy.start()
    copy.wait()


def put_call(where, rows, earlier, part, tile_cols):
    far = pl.BlockSpec(memory_space=pl.ANY)
    return pl.pallas_call(
        functools.partial(put_kernel, part, tile_cols),
        in_specs=[pl.BlockSpec(memory_space=pltpu.SMEM), pl.BlockSpec(memory_space=pltpu.VMEM), far],
        out_specs=far,
        out_shape=jax.ShapeDtypeStruct(earlier.shape, earlier.dtype),
        scratch_shapes=[pltpu.SemaphoreType.DMA],
        input_output_aliases={2: 0},
        compiler_params=pltpu.CompilerParams(vmem_limit_bytes=VMEM_LIMIT),
        cost_estimate=pl.CostEstimate(flops=0, bytes_accessed=2 * 2**20, transcendentals=0),
        name="put",
    )(where, rows, earlier)


def shards(
    alignment_left,
    alignment_right,
    pair_features,
    output_weight,
    output_bias,
    norm_scale_gain,
    projection_weight,
    gate_offset_bias,
):
    parts, cols = lax.axis_size("row"), lax.axis_size("col")
    line = cols // CORES
    assert line == parts
    tile_rows, tile_cols, channels = pair_features.shape
    row, col = lax.axis_index("row"), lax.axis_index("col")
    where = jnp.stack([row, col // CORES, col % CORES]).astype(jnp.int32)

    rights = [alignment_right]
    for d in range(1, parts):
        rights.append(lax.ppermute(alignment_right, "row", [(a, a ^ d) for a in range(parts)]))
    left = lax.all_gather(alignment_left, "col", axis=0, tiled=True)

    weight = output_weight.T
    bias = output_bias.reshape(channels, 1)
    gain = norm_scale_gain.reshape(channels, 1)

    total = projection_weight.shape[1]
    group = total // cols
    gate_start = total - gate_offset_bias.shape[0]
    turned = projection_weight.T
    offsets = jnp.concatenate([jnp.zeros((gate_start,), jnp.float32), gate_offset_bias]).reshape(total, 1)
    gates = (jnp.arange(total) >= gate_start).astype(jnp.float32).reshape(total, 1)

    def chosen(array):
        return jnp.concatenate(
            [lax.dynamic_slice_in_dim(array, (col ^ e) * group, group, 0) for e in range(CORES)], axis=0
        )

    my_weight, my_offsets, my_gates = chosen(turned), chosen(offsets), chosen(gates)

    count = tile_cols // STEP
    state = {"new_pair": None, "result": None}
    tiles = [{} for _ in range(count)]
    moved = [None] * count
    handed = [None] * count

    def after(value, *others):
        return lax.optimization_barrier((value, others))[0]

    def update(part, *others):
        state["new_pair"], tiles[part][0] = update_call(
            after(where, *others), left, rights, pair_features, weight, bias, gain, state["new_pair"], part
        )

    ring = [z * CORES for z in range(line)] + [z * CORES + 1 for z in reversed(range(line))]
    onward = [(ring[t], ring[(t + 1) % cols]) for t in range(cols)]
    back = [(b, a) for a, b in onward]

    def shift(part, s, *others):
        here = tiles[part]
        here[-s] = lax.ppermute(after(here[-(s - 1)], *others), "col", onward)
        here[s] = lax.ppermute(after(here[s - 1], *others), "col", back)

    def project(part, *others):
        here = tiles[part]
        moved[part] = list(
            project_call(
                after(where, *others),
                my_weight,
                my_offsets,
                my_gates,
                [here[o] for o in range(-(line - 1), line)],
                parts,
            )
        )

    def send(part, d):
        piece = moved[part][d]
        if d > 2 and part < count - 1:
            piece = after(piece, moved[part][1], moved[part][2])
        moved[part][d] = lax.ppermute(piece, "row", [(a, a ^ d) for a in range(parts)])

    def place(part, *others):
        state["result"], handed[part] = place_call(
            after(where, *others), moved[part], state["result"], part, parts, tile_cols
        )
        swapped[part] = lax.ppermute(handed[part], "col", [(c, c ^ 1) for c in range(cols)])

    def put(part):
        state["result"] = put_call(where, swapped[part], state["result"], part, tile_cols)

    steps = line - 1
    swapped = [None] * count
    gate, before = [], []

    def last(part):
        return steps * (part + 1) - 1

    update(0)
    for index in range(count * steps):
        shift(index // steps, index % steps + 1, *gate)
        here = tiles[index // steps]
        gate = [here[-(index % steps + 1)], here[index % steps + 1]]
        now = list(gate)
        if index + 1 < count:
            update(index + 1, *before)
            gate.append(tiles[index + 1][0])
        for part in range(count - 1):
            if index == last(part) + 1:
                project(part, *before)
                gate.append(moved[part][0])
                for d in range(1, parts):
                    send(part, d)
            if index == last(part) + 2:
                gate += moved[part][1:3]
            if index == last(part) + 5:
                place(part, *before)
                gate.append(handed[part])
            if index == last(part) + 6:
                gate.append(swapped[part])
                put(part)
        before = now
    project(count - 1)
    for d in range(1, parts):
        send(count - 1, d)
    for part in range(count):
        if swapped[part] is None:
            place(part)
            put(part)
    return (state["new_pair"], state["result"])


def solution(mesh):
    placed = (
        P(("row", "col"), None),
        P("row", "col"),
        P("row", "col", None),
        P(),
        P(),
        P(),
        P(),
        P(),
    )
    return jax.shard_map(
        shards,
        mesh=mesh,
        in_specs=placed,
        out_specs=(P("row", "col", None), P("row", "col", None)),
        check_vma=False,
    )
```

```python
import functools

import jax
import jax.numpy as jnp
from jax import lax
from jax.experimental import pallas as pl
from jax.experimental.pallas import tpu as pltpu
from jax.sharding import PartitionSpec as P

CHANNEL_WIDTH = 32
CORES = 2
STEP = 16
VMEM_LIMIT = 50 * 1024 * 1024

norm_eps = 1e-05

NT = (((1,), (1,)), ((), ()))


def update_kernel(
    parts,
    part,
    where_ref,
    left_ref,
    *refs,
):
    rights = refs[:parts]
    pair_ref, weight_ref, bias_ref, gain_ref = refs[parts : parts + 4]
    new_ref, normed_ref, right_all, right_turned, outer, rows, sems = refs[-7:]
    tile_rows = pair_ref.shape[0]
    share = rights[0].shape[0]
    depth = share * parts
    width = STEP * CHANNEL_WIDTH
    mine = where_ref[0]
    copies = []
    for d in range(parts):
        source = rights[d].at[:, pl.ds(part * width, width)]
        place = pl.multiple_of((mine ^ d) * share, share)
        copy = pltpu.make_async_copy(source, right_all.at[pl.ds(place, share), :], sems.at[d])
        copy.start()
        copies.append(copy)
    rows[...] = pair_ref[...].astype(jnp.float32).reshape(tile_rows * STEP, -1)
    for copy in copies:
        copy.wait()
    right_turned[...] = right_all[...].T
    for c1 in range(0, CHANNEL_WIDTH, 2):
        both = jnp.concatenate(
            [left_ref[:, c * depth : (c + 1) * depth] for c in (c1, c1 + 1)], axis=0
        )
        product = lax.dot_general(right_turned[...], both, NT, preferred_element_type=jnp.float32)
        outer[:, c1 * tile_rows : (c1 + 2) * tile_rows] = (product * (1.0 / depth)).astype(jnp.bfloat16)
    for j in range(0, STEP, 2):
        columns = [
            jnp.concatenate(
                [
                    outer[
                        jj * CHANNEL_WIDTH : (jj + 1) * CHANNEL_WIDTH,
                        c1 * tile_rows : (c1 + 1) * tile_rows,
                    ]
                    for c1 in range(CHANNEL_WIDTH)
                ],
                axis=0,
            )
            for jj in (j, j + 1)
        ]
        update = jnp.dot(
            weight_ref[...], jnp.concatenate(columns, axis=1), preferred_element_type=jnp.float32
        )
        for jj in (j, j + 1):
            mine_update = update[:, (jj - j) * tile_rows : (jj - j + 1) * tile_rows] + bias_ref[...]
            place = pl.ds(jj, tile_rows, stride=STEP)
            fresh = rows[place, :].T + mine_update
            widened = fresh.astype(jnp.bfloat16).astype(jnp.float32)
            rows[place, :] = widened.T
            centred = widened - jnp.mean(widened, axis=0, keepdims=True)
            variance = jnp.mean(centred * centred, axis=0, keepdims=True)
            normed_ref[jj] = (centred * lax.rsqrt(variance + norm_eps) * gain_ref[...]).astype(jnp.bfloat16)
    new_ref[...] = rows[...].reshape(tile_rows, STEP, -1).astype(jnp.bfloat16)


def update_call(where, left, rights, pair, weight, bias, gain, earlier, part):
    tile_rows, tile_cols, channels = pair.shape
    parts = len(rights)
    depth = rights[0].shape[0] * parts
    width = STEP * CHANNEL_WIDTH
    whole = pl.BlockSpec(memory_space=pltpu.VMEM)
    far = pl.BlockSpec(memory_space=pl.ANY)
    block = pl.BlockSpec((tile_rows, STEP, channels), lambda g: (0, part, 0))
    args = [where, left, *rights, pair, weight, bias, gain]
    specs = [
        pl.BlockSpec(memory_space=pltpu.SMEM),
        whole,
        *[far] * parts,
        block,
        whole,
        whole,
        whole,
    ]
    aliases = {}
    if earlier is not None:
        aliases = {len(args): 0}
        args.append(earlier)
        specs.append(far)
    flops = 2 * width * CHANNEL_WIDTH * tile_rows * depth + 2 * STEP * tile_rows * CHANNEL_WIDTH**2 * channels
    return pl.pallas_call(
        functools.partial(update_kernel, parts, part),
        grid=(1,),
        in_specs=specs,
        out_specs=(block, pl.BlockSpec((STEP, channels, tile_rows), lambda g: (0, 0, 0))),
        out_shape=(
            jax.ShapeDtypeStruct(pair.shape, jnp.bfloat16),
            jax.ShapeDtypeStruct((STEP, channels, tile_rows), jnp.bfloat16),
        ),
        scratch_shapes=[
            pltpu.VMEM((depth, width), jnp.bfloat16),
            pltpu.VMEM((width, depth), jnp.bfloat16),
            pltpu.VMEM((width, CHANNEL_WIDTH * tile_rows), jnp.bfloat16),
            pltpu.VMEM((tile_rows * STEP, channels), jnp.float32),
            pltpu.SemaphoreType.DMA((parts,)),
        ],
        input_output_aliases=aliases,
        compiler_params=pltpu.CompilerParams(vmem_limit_bytes=VMEM_LIMIT),
        cost_estimate=pl.CostEstimate(flops=flops, bytes_accessed=8 * 2**20, transcendentals=0),
        name="update",
    )(*args)


def project_kernel(line, parts, where_ref, weight_ref, offset_ref, gate_ref, *refs):
    tiles = refs[: 2 * line - 1]
    outs = refs[2 * line - 1 : 2 * line - 1 + parts]
    held, sems = refs[-2:]
    mine, place, core = where_ref[0], where_ref[1], where_ref[2]
    group = weight_ref.shape[0] // CORES
    lanes = held.shape[-1]

    def fetch(d):
        distance = ((mine ^ d) - place) * (1 - 2 * core)
        for index in range(2 * line - 1):
            @pl.when(distance == index - (line - 1))
            def _():
                pltpu.make_async_copy(tiles[index], held.at[d % 2], sems.at[d % 2]).start()

    fetch(0)
    for d in range(parts):
        if d + 1 < parts:
            fetch(d + 1)
        pltpu.make_async_copy(tiles[0], held.at[d % 2], sems.at[d % 2]).wait()
        for j in range(0, STEP, 2):
            both = jnp.concatenate([held[d % 2, j], held[d % 2, j + 1]], axis=1)
            raw = jnp.dot(weight_ref[...], both, preferred_element_type=jnp.float32)
            gated = 1.0 / (1.0 + jnp.exp(-(raw + offset_ref[...])))
            result = jnp.where(gate_ref[...] > 0.0, gated, raw).astype(jnp.bfloat16)
            for e in range(CORES):
                for jj in range(2):
                    outs[d][e, j + jj] = result[e * group : (e + 1) * group, jj * lanes : (jj + 1) * lanes]


def project_call(where, weight, offset, gate, tiles, parts):
    line = (len(tiles) + 1) // 2
    channels, lanes = tiles[0].shape[1:]
    group = weight.shape[0] // CORES
    whole = pl.BlockSpec(memory_space=pltpu.VMEM)
    far = pl.BlockSpec(memory_space=pl.ANY)
    shape = jax.ShapeDtypeStruct((CORES, STEP, group, lanes), jnp.bfloat16)
    return pl.pallas_call(
        functools.partial(project_kernel, line, parts),
        in_specs=[pl.BlockSpec(memory_space=pltpu.SMEM), whole, whole, whole, *[far] * len(tiles)],
        out_specs=[whole] * parts,
        out_shape=[shape] * parts,
        scratch_shapes=[
            pltpu.VMEM((2, STEP, channels, lanes), jnp.bfloat16),
            pltpu.SemaphoreType.DMA((2,)),
        ],
        compiler_params=pltpu.CompilerParams(vmem_limit_bytes=VMEM_LIMIT),
        cost_estimate=pl.CostEstimate(
            flops=2 * parts * STEP * channels * lanes * weight.shape[0],
            bytes_accessed=4 * 2**20,
            transcendentals=0,
        ),
        name="project",
    )(where, weight, offset, gate, *tiles)


def place_kernel(parts, part, tile_cols, where_ref, *refs):
    pieces = refs[:parts]
    out_ref, other_ref, rows, sem = refs[-4:]
    mine, core = where_ref[0], where_ref[2]
    step, group, lanes = pieces[0].shape[1:]
    for e, target in enumerate((rows, other_ref)):
        for d in range(parts):
            column = pl.multiple_of((mine ^ d) * lanes, lanes)
            target[:, :, pl.ds(column, lanes)] = pieces[d][e]
        if e == 0:
            row = pl.multiple_of(core * tile_cols + part * step, step)
            copy = pltpu.make_async_copy(rows, out_ref.at[pl.ds(row, step)], sem)
            copy.start()
    copy.wait()


def place_call(where, pieces, earlier, part, parts, tile_cols):
    step, group, lanes = pieces[0].shape[1:]
    far = pl.BlockSpec(memory_space=pl.ANY)
    whole = pl.BlockSpec(memory_space=pltpu.VMEM)
    args = [where, *pieces]
    specs = [pl.BlockSpec(memory_space=pltpu.SMEM), *[whole] * len(pieces)]
    aliases = {}
    if earlier is not None:
        aliases = {len(args): 0}
        args.append(earlier)
        specs.append(far)
    block = (step, group, parts * lanes)
    return pl.pallas_call(
        functools.partial(place_kernel, parts, part, tile_cols),
        in_specs=specs,
        out_specs=(far, whole),
        out_shape=(
            jax.ShapeDtypeStruct((CORES * tile_cols, *block[1:]), jnp.bfloat16),
            jax.ShapeDtypeStruct(block, jnp.bfloat16),
        ),
        scratch_shapes=[pltpu.VMEM(block, jnp.bfloat16), pltpu.SemaphoreType.DMA],
        input_output_aliases=aliases,
        compiler_params=pltpu.CompilerParams(vmem_limit_bytes=VMEM_LIMIT),
        cost_estimate=pl.CostEstimate(flops=0, bytes_accessed=6 * 2**20, transcendentals=0),
        name="place",
    )(*args)


def put_kernel(part, tile_cols, where_ref, rows_ref, earlier_ref, out_ref, sem):
    del earlier_ref
    row = pl.multiple_of((1 - where_ref[2]) * tile_cols + part * rows_ref.shape[0], rows_ref.shape[0])
    copy = pltpu.make_async_copy(rows_ref, out_ref.at[pl.ds(row, rows_ref.shape[0])], sem)
    copy.start()
    copy.wait()


def put_call(where, rows, earlier, part, tile_cols):
    far = pl.BlockSpec(memory_space=pl.ANY)
    return pl.pallas_call(
        functools.partial(put_kernel, part, tile_cols),
        in_specs=[pl.BlockSpec(memory_space=pltpu.SMEM), pl.BlockSpec(memory_space=pltpu.VMEM), far],
        out_specs=far,
        out_shape=jax.ShapeDtypeStruct(earlier.shape, earlier.dtype),
        scratch_shapes=[pltpu.SemaphoreType.DMA],
        input_output_aliases={2: 0},
        compiler_params=pltpu.CompilerParams(vmem_limit_bytes=VMEM_LIMIT),
        cost_estimate=pl.CostEstimate(flops=0, bytes_accessed=2 * 2**20, transcendentals=0),
        name="put",
    )(where, rows, earlier)


def shards(
    alignment_left,
    alignment_right,
    pair_features,
    output_weight,
    output_bias,
    norm_scale_gain,
    projection_weight,
    gate_offset_bias,
):
    parts, cols = lax.axis_size("row"), lax.axis_size("col")
    line = cols // CORES
    assert line == parts
    tile_rows, tile_cols, channels = pair_features.shape
    row, col = lax.axis_index("row"), lax.axis_index("col")
    where = jnp.stack([row, col // CORES, col % CORES]).astype(jnp.int32)

    rights = [alignment_right]
    for d in range(1, parts):
        rights.append(lax.ppermute(alignment_right, "row", [(a, a ^ d) for a in range(parts)]))
    left = lax.all_gather(alignment_left, "col", axis=0, tiled=True)

    weight = output_weight.T
    bias = output_bias.reshape(channels, 1)
    gain = norm_scale_gain.reshape(channels, 1)

    total = projection_weight.shape[1]
    group = total // cols
    gate_start = total - gate_offset_bias.shape[0]
    turned = projection_weight.T
    offsets = jnp.concatenate([jnp.zeros((gate_start,), jnp.float32), gate_offset_bias]).reshape(total, 1)
    gates = (jnp.arange(total) >= gate_start).astype(jnp.float32).reshape(total, 1)

    def chosen(array):
        return jnp.concatenate(
            [lax.dynamic_slice_in_dim(array, (col ^ e) * group, group, 0) for e in range(CORES)], axis=0
        )

    my_weight, my_offsets, my_gates = chosen(turned), chosen(offsets), chosen(gates)

    count = tile_cols // STEP
    state = {"new_pair": None, "result": None}
    tiles = [{} for _ in range(count)]
    moved = [None] * count
    handed = [None] * count

    def after(value, *others):
        return lax.optimization_barrier((value, others))[0]

    def update(part, *others):
        state["new_pair"], tiles[part][0] = update_call(
            after(where, *others), left, rights, pair_features, weight, bias, gain, state["new_pair"], part
        )

    ring = [z * CORES for z in range(line)] + [z * CORES + 1 for z in reversed(range(line))]
    onward = [(ring[t], ring[(t + 1) % cols]) for t in range(cols)]
    back = [(b, a) for a, b in onward]

    def shift(part, s, *others):
        here = tiles[part]
        here[-s] = lax.ppermute(after(here[-(s - 1)], *others), "col", onward)
        here[s] = lax.ppermute(after(here[s - 1], *others), "col", back)

    def project(part, *others):
        here = tiles[part]
        moved[part] = list(
            project_call(
                after(where, *others),
                my_weight,
                my_offsets,
                my_gates,
                [here[o] for o in range(-(line - 1), line)],
                parts,
            )
        )

    def send(part, d, *others):
        piece = after(moved[part][d], *others)
        moved[part][d] = lax.ppermute(piece, "row", [(a, a ^ d) for a in range(parts)])

    def place(part, *others):
        state["result"], handed[part] = place_call(
            after(where, *others), moved[part], state["result"], part, parts, tile_cols
        )

    def exchange(part, *others):
        handed[part] = after(handed[part], *others)
        swapped[part] = lax.ppermute(handed[part], "col", [(c, c ^ 1) for c in range(cols)])

    def put(part):
        state["result"] = put_call(where, swapped[part], state["result"], part, tile_cols)

    order = sorted(
        ((part, s) for part in range(count) for s in range(1, line)),
        key=lambda step: (step[0] + step[1], step[0]),
    )
    first = [order.index((part, 1)) for part in range(count)]
    last = [order.index((part, line - 1)) for part in range(count)]
    gates = [[] for _ in range(len(order) + 2)]
    swapped = [None] * count
    done = []

    update(0)
    for index, (part, s) in enumerate(order):
        shift(part, s, *gates[index])
        done.append([tiles[part][-s], tiles[part][s]])
        gates[index + 2] += done[index]
        before = done[index - 1] if index else []
        for p in range(1, count):
            if index == max(0, first[p] - 2):
                update(p, *before)
                gates[index + 2].append(tiles[p][0])
        for p in range(count - 1):
            if index == last[p] + 1:
                project(p, *before)
                gates[min(index + 2, len(order) - 1)].append(moved[p][0])
            for d in range(1, parts):
                if index == last[p] + d and p < count - 2:
                    send(p, d, *before)
                    gates[index + 2].append(moved[p][d])
            if p < count - 2 and index == min(last[p] + parts + 1, len(order) - 1):
                place(p, *before)
                gates[min(index + 2, len(order) - 1)].append(handed[p])
    for d in range(1, parts):
        send(count - 2, d, *(moved[count - 2][1:3] if d > 2 else []))
    project(count - 1, *moved[count - 2][1:])
    for d in range(1, parts):
        send(count - 1, d)
    place(count - 2)
    place(count - 1, *handed[:-1])
    for part in range(count):
        exchange(part, *moved[-1][1:])
        put(part)
    return (state["new_pair"], state["result"])


def solution(mesh):
    placed = (
        P(("row", "col"), None),
        P("row", "col"),
        P("row", "col", None),
        P(),
        P(),
        P(),
        P(),
        P(),
    )
    return jax.shard_map(
        shards,
        mesh=mesh,
        in_specs=placed,
        out_specs=(P("row", "col", None), P("row", "col", None)),
        check_vma=False,
    )
```

```python
import functools

import jax
import jax.numpy as jnp
from jax import lax
from jax.experimental import pallas as pl
from jax.experimental.pallas import tpu as pltpu
from jax.sharding import PartitionSpec as P

CHANNEL_WIDTH = 32
CORES = 2
STEP = 16
VMEM_LIMIT = 50 * 1024 * 1024

norm_eps = 1e-05

NT = (((1,), (1,)), ((), ()))


def update_kernel(
    parts,
    part,
    cols,
    plan,
    where_ref,
    *refs,
):
    lefts, refs = refs[: len(plan)], refs[len(plan) :]
    rights = refs[:parts]
    pair_ref, weight_ref, bias_ref, gain_ref = refs[parts : parts + 4]
    new_ref, normed_ref, left_ref, right_all, right_turned, outer, rows, sems = refs[-8:]
    tile_rows = pair_ref.shape[0]
    share = rights[0].shape[0]
    depth = share * parts
    width = STEP * CHANNEL_WIDTH
    mine = where_ref[0]
    copies = []
    for d in range(parts):
        source = rights[d].at[:, pl.ds(part * width, width)]
        place = pl.multiple_of((mine ^ d) * share, share)
        copy = pltpu.make_async_copy(source, right_all.at[pl.ds(place, share), :], sems.at[d])
        copy.start()
        copies.append(copy)
    chip, core = where_ref[1], where_ref[2]
    spot = chip + core * (cols - 1 - 2 * chip)
    for n, (offset, column) in enumerate(plan):
        height, length = lefts[n].shape
        row = 0
        if offset is not None:
            owner = lax.rem(spot + offset + cols, cols)
            owner = jnp.where(owner < cols // 2, CORES * owner, CORES * (cols - 1 - owner) + 1)
            row = pl.multiple_of(owner * height, height)
        target = left_ref.at[pl.ds(row, height), pl.ds(column, length)]
        copy = pltpu.make_async_copy(lefts[n], target, sems.at[parts + n])
        copy.start()
        copies.append(copy)
    rows[...] = pair_ref[...].astype(jnp.float32).reshape(tile_rows * STEP, -1)
    for copy in copies[:parts]:
        copy.wait()
    right_turned[...] = right_all[...].T
    for copy in copies[parts:]:
        copy.wait()
    for c1 in range(0, CHANNEL_WIDTH, 2):
        both = jnp.concatenate(
            [left_ref[:, c * depth : (c + 1) * depth] for c in (c1, c1 + 1)], axis=0
        )
        product = lax.dot_general(right_turned[...], both, NT, preferred_element_type=jnp.float32)
        outer[:, c1 * tile_rows : (c1 + 2) * tile_rows] = (product * (1.0 / depth)).astype(jnp.bfloat16)
    for j in range(0, STEP, 2):
        columns = [
            jnp.concatenate(
                [
                    outer[
                        jj * CHANNEL_WIDTH : (jj + 1) * CHANNEL_WIDTH,
                        c1 * tile_rows : (c1 + 1) * tile_rows,
                    ]
                    for c1 in range(CHANNEL_WIDTH)
                ],
                axis=0,
            )
            for jj in (j, j + 1)
        ]
        update = jnp.dot(
            weight_ref[...], jnp.concatenate(columns, axis=1), preferred_element_type=jnp.float32
        )
        for jj in (j, j + 1):
            mine_update = update[:, (jj - j) * tile_rows : (jj - j + 1) * tile_rows] + bias_ref[...]
            place = pl.ds(jj, tile_rows, stride=STEP)
            fresh = rows[place, :].T + mine_update
            widened = fresh.astype(jnp.bfloat16).astype(jnp.float32)
            rows[place, :] = widened.T
            centred = widened - jnp.mean(widened, axis=0, keepdims=True)
            variance = jnp.mean(centred * centred, axis=0, keepdims=True)
            normed_ref[jj] = (centred * lax.rsqrt(variance + norm_eps) * gain_ref[...]).astype(jnp.bfloat16)
    new_ref[...] = rows[...].reshape(tile_rows, STEP, -1).astype(jnp.bfloat16)


def update_call(where, lefts, plan, cols, rights, pair, weight, bias, gain, earlier, part):
    tile_rows, tile_cols, channels = pair.shape
    parts = len(rights)
    depth = rights[0].shape[0] * parts
    width = STEP * CHANNEL_WIDTH
    whole = pl.BlockSpec(memory_space=pltpu.VMEM)
    far = pl.BlockSpec(memory_space=pl.ANY)
    block = pl.BlockSpec((tile_rows, STEP, channels), lambda g: (0, part, 0))
    args = [where, *lefts, *rights, pair, weight, bias, gain]
    specs = [
        pl.BlockSpec(memory_space=pltpu.SMEM),
        *[far] * (len(lefts) + parts),
        block,
        whole,
        whole,
        whole,
    ]
    aliases = {}
    if earlier is not None:
        aliases = {len(args): 0}
        args.append(earlier)
        specs.append(far)
    flops = 2 * width * CHANNEL_WIDTH * tile_rows * depth + 2 * STEP * tile_rows * CHANNEL_WIDTH**2 * channels
    return pl.pallas_call(
        functools.partial(update_kernel, parts, part, cols, plan),
        grid=(1,),
        in_specs=specs,
        out_specs=(block, pl.BlockSpec((STEP, channels, tile_rows), lambda g: (0, 0, 0))),
        out_shape=(
            jax.ShapeDtypeStruct(pair.shape, jnp.bfloat16),
            jax.ShapeDtypeStruct((STEP, channels, tile_rows), jnp.bfloat16),
        ),
        scratch_shapes=[
            pltpu.VMEM((tile_rows, CHANNEL_WIDTH * depth), jnp.bfloat16),
            pltpu.VMEM((depth, width), jnp.bfloat16),
            pltpu.VMEM((width, depth), jnp.bfloat16),
            pltpu.VMEM((width, CHANNEL_WIDTH * tile_rows), jnp.bfloat16),
            pltpu.VMEM((tile_rows * STEP, channels), jnp.float32),
            pltpu.SemaphoreType.DMA((parts + len(plan),)),
        ],
        input_output_aliases=aliases,
        compiler_params=pltpu.CompilerParams(vmem_limit_bytes=VMEM_LIMIT),
        cost_estimate=pl.CostEstimate(flops=flops, bytes_accessed=8 * 2**20, transcendentals=0),
        name="update",
    )(*args)


def project_kernel(line, parts, where_ref, weight_ref, offset_ref, gate_ref, *refs):
    tiles = refs[: 2 * line - 1]
    outs = refs[2 * line - 1 : 2 * line - 1 + parts]
    held, sems = refs[-2:]
    mine, place, core = where_ref[0], where_ref[1], where_ref[2]
    group = weight_ref.shape[0] // CORES
    lanes = held.shape[-1]

    def fetch(d):
        distance = ((mine ^ d) - place) * (1 - 2 * core)
        for index in range(2 * line - 1):
            @pl.when(distance == index - (line - 1))
            def _():
                pltpu.make_async_copy(tiles[index], held.at[d % 2], sems.at[d % 2]).start()

    fetch(0)
    for d in range(parts):
        if d + 1 < parts:
            fetch(d + 1)
        pltpu.make_async_copy(tiles[0], held.at[d % 2], sems.at[d % 2]).wait()
        for j in range(0, STEP, 2):
            both = jnp.concatenate([held[d % 2, j], held[d % 2, j + 1]], axis=1)
            raw = jnp.dot(weight_ref[...], both, preferred_element_type=jnp.float32)
            gated = 1.0 / (1.0 + jnp.exp(-(raw + offset_ref[...])))
            result = jnp.where(gate_ref[...] > 0.0, gated, raw).astype(jnp.bfloat16)
            for e in range(CORES):
                for jj in range(2):
                    outs[d][e, j + jj] = result[e * group : (e + 1) * group, jj * lanes : (jj + 1) * lanes]


def project_call(where, weight, offset, gate, tiles, parts):
    line = (len(tiles) + 1) // 2
    channels, lanes = tiles[0].shape[1:]
    group = weight.shape[0] // CORES
    whole = pl.BlockSpec(memory_space=pltpu.VMEM)
    far = pl.BlockSpec(memory_space=pl.ANY)
    shape = jax.ShapeDtypeStruct((CORES, STEP, group, lanes), jnp.bfloat16)
    return pl.pallas_call(
        functools.partial(project_kernel, line, parts),
        in_specs=[pl.BlockSpec(memory_space=pltpu.SMEM), whole, whole, whole, *[far] * len(tiles)],
        out_specs=[whole] * parts,
        out_shape=[shape] * parts,
        scratch_shapes=[
            pltpu.VMEM((2, STEP, channels, lanes), jnp.bfloat16),
            pltpu.SemaphoreType.DMA((2,)),
        ],
        compiler_params=pltpu.CompilerParams(vmem_limit_bytes=VMEM_LIMIT),
        cost_estimate=pl.CostEstimate(
            flops=2 * parts * STEP * channels * lanes * weight.shape[0],
            bytes_accessed=4 * 2**20,
            transcendentals=0,
        ),
        name="project",
    )(where, weight, offset, gate, *tiles)


def place_kernel(parts, part, tile_cols, where_ref, *refs):
    pieces = refs[:parts]
    out_ref, other_ref, rows, sem = refs[-4:]
    mine, core = where_ref[0], where_ref[2]
    step, group, lanes = pieces[0].shape[1:]
    for e, target in enumerate((rows, other_ref)):
        for d in range(parts):
            column = pl.multiple_of((mine ^ d) * lanes, lanes)
            target[:, :, pl.ds(column, lanes)] = pieces[d][e]
        if e == 0:
            row = pl.multiple_of(core * tile_cols + part * step, step)
            copy = pltpu.make_async_copy(rows, out_ref.at[pl.ds(row, step)], sem)
            copy.start()
    copy.wait()


def place_call(where, pieces, earlier, part, parts, tile_cols):
    step, group, lanes = pieces[0].shape[1:]
    far = pl.BlockSpec(memory_space=pl.ANY)
    whole = pl.BlockSpec(memory_space=pltpu.VMEM)
    args = [where, *pieces]
    specs = [pl.BlockSpec(memory_space=pltpu.SMEM), *[whole] * len(pieces)]
    aliases = {}
    if earlier is not None:
        aliases = {len(args): 0}
        args.append(earlier)
        specs.append(far)
    block = (step, group, parts * lanes)
    return pl.pallas_call(
        functools.partial(place_kernel, parts, part, tile_cols),
        in_specs=specs,
        out_specs=(far, whole),
        out_shape=(
            jax.ShapeDtypeStruct((CORES * tile_cols, *block[1:]), jnp.bfloat16),
            jax.ShapeDtypeStruct(block, jnp.bfloat16),
        ),
        scratch_shapes=[pltpu.VMEM(block, jnp.bfloat16), pltpu.SemaphoreType.DMA],
        input_output_aliases=aliases,
        compiler_params=pltpu.CompilerParams(vmem_limit_bytes=VMEM_LIMIT),
        cost_estimate=pl.CostEstimate(flops=0, bytes_accessed=6 * 2**20, transcendentals=0),
        name="place",
    )(*args)


def put_kernel(tile_cols, where_ref, *refs):
    out_ref, sems = refs[-2:]
    copies = []
    for part, rows_ref in enumerate(refs[:-3]):
        step = rows_ref.shape[0]
        row = pl.multiple_of((1 - where_ref[2]) * tile_cols + part * step, step)
        copy = pltpu.make_async_copy(rows_ref, out_ref.at[pl.ds(row, step)], sems.at[part])
        copy.start()
        copies.append(copy)
    for copy in copies:
        copy.wait()


def put_call(where, rows, earlier, tile_cols):
    far = pl.BlockSpec(memory_space=pl.ANY)
    whole = pl.BlockSpec(memory_space=pltpu.VMEM)
    return pl.pallas_call(
        functools.partial(put_kernel, tile_cols),
        in_specs=[pl.BlockSpec(memory_space=pltpu.SMEM), *[whole] * len(rows), far],
        out_specs=far,
        out_shape=jax.ShapeDtypeStruct(earlier.shape, earlier.dtype),
        scratch_shapes=[pltpu.SemaphoreType.DMA((len(rows),))],
        input_output_aliases={1 + len(rows): 0},
        compiler_params=pltpu.CompilerParams(vmem_limit_bytes=VMEM_LIMIT),
        cost_estimate=pl.CostEstimate(flops=0, bytes_accessed=8 * 2**20, transcendentals=0),
        name="put",
    )(where, *rows, earlier)


def shards(
    alignment_left,
    alignment_right,
    pair_features,
    output_weight,
    output_bias,
    norm_scale_gain,
    projection_weight,
    gate_offset_bias,
):
    parts, cols = lax.axis_size("row"), lax.axis_size("col")
    line = cols // CORES
    assert line == parts
    tile_rows, tile_cols, channels = pair_features.shape
    row, col = lax.axis_index("row"), lax.axis_index("col")
    where = jnp.stack([row, col // CORES, col % CORES]).astype(jnp.int32)

    rights = [alignment_right]
    for d in range(1, parts):
        rights.append(lax.ppermute(alignment_right, "row", [(a, a ^ d) for a in range(parts)]))

    ring = [z * CORES for z in range(line)] + [z * CORES + 1 for z in reversed(range(line))]
    onward = [(ring[t], ring[(t + 1) % cols]) for t in range(cols)]
    back = [(b, a) for a, b in onward]

    if alignment_left.shape[0] % 16 == 0:
        held = {0: alignment_left}
        for s in range(1, line):
            ahead, behind = held[-(s - 1)], held[s - 1]
            if s == line - 1:
                ahead, behind, _ = lax.optimization_barrier((ahead, behind, rights[1:]))
            held[-s] = lax.ppermute(ahead, "col", onward)
            held[s] = lax.ppermute(behind, "col", back)
        half = alignment_left.shape[1] // 2
        plan = tuple((offset, 0) for offset in sorted(held)) + ((line, 0), (line, half))
        lefts = [held[offset] for offset in sorted(held)]
        lefts.append(lax.ppermute(held[1 - line][:, :half], "col", onward))
        lefts.append(lax.ppermute(held[line - 1][:, half:], "col", back))
    else:
        plan = ((None, 0),)
        lefts = [lax.all_gather(alignment_left, "col", axis=0, tiled=True)]

    weight = output_weight.T
    bias = output_bias.reshape(channels, 1)
    gain = norm_scale_gain.reshape(channels, 1)

    total = projection_weight.shape[1]
    group = total // cols
    gate_start = total - gate_offset_bias.shape[0]
    turned = projection_weight.T
    offsets = jnp.concatenate([jnp.zeros((gate_start,), jnp.float32), gate_offset_bias]).reshape(total, 1)
    gates = (jnp.arange(total) >= gate_start).astype(jnp.float32).reshape(total, 1)

    def chosen(array):
        return jnp.concatenate(
            [lax.dynamic_slice_in_dim(array, (col ^ e) * group, group, 0) for e in range(CORES)], axis=0
        )

    my_weight, my_offsets, my_gates = chosen(turned), chosen(offsets), chosen(gates)

    count = tile_cols // STEP
    state = {"new_pair": None, "result": None}
    tiles = [{} for _ in range(count)]
    moved = [None] * count
    handed = [None] * count

    def after(value, *others):
        return lax.optimization_barrier((value, others))[0]

    def update(part, *others):
        state["new_pair"], tiles[part][0] = update_call(
            after(where, *others),
            lefts,
            plan,
            cols,
            rights,
            pair_features,
            weight,
            bias,
            gain,
            state["new_pair"],
            part,
        )

    def shift(part, s, *others):
        here = tiles[part]
        here[-s] = lax.ppermute(after(here[-(s - 1)], *others), "col", onward)
        here[s] = lax.ppermute(after(here[s - 1], *others), "col", back)

    def project(part, *others):
        here = tiles[part]
        moved[part] = list(
            project_call(
                after(where, *others),
                my_weight,
                my_offsets,
                my_gates,
                [here[o] for o in range(-(line - 1), line)],
                parts,
            )
        )

    def send(part, d, *others):
        piece = after(moved[part][d], *others)
        moved[part][d] = lax.ppermute(piece, "row", [(a, a ^ d) for a in range(parts)])

    def place(part, *others):
        state["result"], handed[part] = place_call(
            after(where, *others), moved[part], state["result"], part, parts, tile_cols
        )

    def exchange(part, *others):
        handed[part] = after(handed[part], *others)
        swapped[part] = lax.ppermute(handed[part], "col", [(c, c ^ 1) for c in range(cols)])

    order = sorted(
        ((part, s) for part in range(count) for s in range(1, line)),
        key=lambda step: (step[0] + step[1], step[0]),
    )
    first = [order.index((part, 1)) for part in range(count)]
    last = [order.index((part, line - 1)) for part in range(count)]
    gates = [[] for _ in range(len(order) + 2)]
    swapped = [None] * count
    done = []

    update(0)
    for index, (part, s) in enumerate(order):
        shift(part, s, *gates[index])
        done.append([tiles[part][-s], tiles[part][s]])
        gates[index + 2] += done[index]
        before = done[index - 1] if index else []
        for p in range(1, count):
            if index == max(0, first[p] - 2):
                update(p, *before)
                gates[index + 2].append(tiles[p][0])
        for p in range(count - 1):
            if index == last[p] + 1:
                project(p, *before)
                gates[min(index + 2, len(order) - 1)].append(moved[p][0])
            for d in range(1, parts):
                if index == last[p] + d and p < count - 2:
                    send(p, d, *before)
                    gates[index + 2].append(moved[p][d])
            if p < count - 2 and index == min(last[p] + parts + 1, len(order) - 1):
                place(p, *before)
                gates[min(index + 2, len(order) - 1)].append(handed[p])
    for d in range(1, parts):
        send(count - 2, d, *(moved[count - 2][1:3] if d > 2 else []))
    project(count - 1, *moved[count - 2][1:])
    for d in range(1, parts):
        send(count - 1, d)
    place(count - 2)
    place(count - 1, *handed[:-1])
    for part in range(count):
        exchange(part, *moved[-1][1:])
    state["result"] = put_call(where, swapped, state["result"], tile_cols)
    return (state["new_pair"], state["result"])


def solution(mesh):
    placed = (
        P(("row", "col"), None),
        P("row", "col"),
        P("row", "col", None),
        P(),
        P(),
        P(),
        P(),
        P(),
    )
    return jax.shard_map(
        shards,
        mesh=mesh,
        in_specs=placed,
        out_specs=(P("row", "col", None), P("row", "col", None)),
        check_vma=False,
    )
```

```python
import functools

import jax
import jax.numpy as jnp
from jax import lax
from jax.experimental import pallas as pl
from jax.experimental.pallas import tpu as pltpu
from jax.sharding import PartitionSpec as P

CHANNEL_WIDTH = 32
CORES = 2
STEP = 16
VMEM_LIMIT = 50 * 1024 * 1024

norm_eps = 1e-05

NT = (((1,), (1,)), ((), ()))


def update_kernel(
    parts,
    part,
    cols,
    plan,
    where_ref,
    *refs,
):
    lefts, refs = refs[: len(plan)], refs[len(plan) :]
    rights = refs[:parts]
    pair_ref, weight_ref, bias_ref, gain_ref = refs[parts : parts + 4]
    new_ref, normed_ref, left_ref, right_all, right_turned, outer, rows, sems = refs[-8:]
    tile_rows = pair_ref.shape[0]
    share = rights[0].shape[0]
    depth = share * parts
    width = STEP * CHANNEL_WIDTH
    mine = where_ref[0]
    copies = []
    for d in range(parts):
        source = rights[d].at[:, pl.ds(part * width, width)]
        place = pl.multiple_of((mine ^ d) * share, share)
        copy = pltpu.make_async_copy(source, right_all.at[pl.ds(place, share), :], sems.at[d])
        copy.start()
        copies.append(copy)
    chip, core = where_ref[1], where_ref[2]
    spot = chip + core * (cols - 1 - 2 * chip)
    for n, (offset, column) in enumerate(plan):
        height, length = lefts[n].shape
        row = 0
        if offset is not None:
            owner = lax.rem(spot + offset + cols, cols)
            owner = jnp.where(owner < cols // 2, CORES * owner, CORES * (cols - 1 - owner) + 1)
            row = pl.multiple_of(owner * height, height)
        target = left_ref.at[pl.ds(row, height), pl.ds(column, length)]
        copy = pltpu.make_async_copy(lefts[n], target, sems.at[parts + n])
        copy.start()
        copies.append(copy)
    rows[...] = pair_ref[...].astype(jnp.float32).reshape(tile_rows * STEP, -1)
    for copy in copies[:parts]:
        copy.wait()
    right_turned[...] = right_all[...].T
    for copy in copies[parts:]:
        copy.wait()
    for c1 in range(0, CHANNEL_WIDTH, 2):
        both = jnp.concatenate(
            [left_ref[:, c * depth : (c + 1) * depth] for c in (c1, c1 + 1)], axis=0
        )
        product = lax.dot_general(right_turned[...], both, NT, preferred_element_type=jnp.float32)
        outer[:, c1 * tile_rows : (c1 + 2) * tile_rows] = (product * (1.0 / depth)).astype(jnp.bfloat16)
    for j in range(0, STEP, 2):
        columns = [
            jnp.concatenate(
                [
                    outer[
                        jj * CHANNEL_WIDTH : (jj + 1) * CHANNEL_WIDTH,
                        c1 * tile_rows : (c1 + 1) * tile_rows,
                    ]
                    for c1 in range(CHANNEL_WIDTH)
                ],
                axis=0,
            )
            for jj in (j, j + 1)
        ]
        update = jnp.dot(
            weight_ref[...], jnp.concatenate(columns, axis=1), preferred_element_type=jnp.float32
        )
        for jj in (j, j + 1):
            mine_update = update[:, (jj - j) * tile_rows : (jj - j + 1) * tile_rows] + bias_ref[...]
            place = pl.ds(jj, tile_rows, stride=STEP)
            fresh = rows[place, :].T + mine_update
            widened = fresh.astype(jnp.bfloat16).astype(jnp.float32)
            rows[place, :] = widened.T
            centred = widened - jnp.mean(widened, axis=0, keepdims=True)
            variance = jnp.mean(centred * centred, axis=0, keepdims=True)
            normed_ref[jj] = (centred * lax.rsqrt(variance + norm_eps) * gain_ref[...]).astype(jnp.bfloat16)
    new_ref[...] = rows[...].reshape(tile_rows, STEP, -1).astype(jnp.bfloat16)


def update_call(where, lefts, plan, cols, rights, pair, weight, bias, gain, earlier, part):
    tile_rows, tile_cols, channels = pair.shape
    parts = len(rights)
    depth = rights[0].shape[0] * parts
    width = STEP * CHANNEL_WIDTH
    whole = pl.BlockSpec(memory_space=pltpu.VMEM)
    far = pl.BlockSpec(memory_space=pl.ANY)
    block = pl.BlockSpec((tile_rows, STEP, channels), lambda g: (0, part, 0))
    args = [where, *lefts, *rights, pair, weight, bias, gain]
    specs = [
        pl.BlockSpec(memory_space=pltpu.SMEM),
        *[far] * (len(lefts) + parts),
        block,
        whole,
        whole,
        whole,
    ]
    aliases = {}
    if earlier is not None:
        aliases = {len(args): 0}
        args.append(earlier)
        specs.append(far)
    flops = 2 * width * CHANNEL_WIDTH * tile_rows * depth + 2 * STEP * tile_rows * CHANNEL_WIDTH**2 * channels
    return pl.pallas_call(
        functools.partial(update_kernel, parts, part, cols, plan),
        grid=(1,),
        in_specs=specs,
        out_specs=(block, pl.BlockSpec((STEP, channels, tile_rows), lambda g: (0, 0, 0))),
        out_shape=(
            jax.ShapeDtypeStruct(pair.shape, jnp.bfloat16),
            jax.ShapeDtypeStruct((STEP, channels, tile_rows), jnp.bfloat16),
        ),
        scratch_shapes=[
            pltpu.VMEM((tile_rows, CHANNEL_WIDTH * depth), jnp.bfloat16),
            pltpu.VMEM((depth, width), jnp.bfloat16),
            pltpu.VMEM((width, depth), jnp.bfloat16),
            pltpu.VMEM((width, CHANNEL_WIDTH * tile_rows), jnp.bfloat16),
            pltpu.VMEM((tile_rows * STEP, channels), jnp.float32),
            pltpu.SemaphoreType.DMA((parts + len(plan),)),
        ],
        input_output_aliases=aliases,
        compiler_params=pltpu.CompilerParams(vmem_limit_bytes=VMEM_LIMIT),
        cost_estimate=pl.CostEstimate(flops=flops, bytes_accessed=8 * 2**20, transcendentals=0),
        name="update",
    )(*args)


def project_kernel(line, parts, where_ref, weight_ref, offset_ref, gate_ref, *refs):
    tiles = refs[: 2 * line - 1]
    outs = refs[2 * line - 1 : 2 * line - 1 + parts]
    held, sems = refs[-2:]
    mine, place, core = where_ref[0], where_ref[1], where_ref[2]
    group = weight_ref.shape[0] // CORES
    lanes = held.shape[-1]

    def fetch(d):
        distance = ((mine ^ d) - place) * (1 - 2 * core)
        for index in range(2 * line - 1):
            @pl.when(distance == index - (line - 1))
            def _():
                pltpu.make_async_copy(tiles[index], held.at[d % 2], sems.at[d % 2]).start()

    fetch(0)
    for d in range(parts):
        if d + 1 < parts:
            fetch(d + 1)
        pltpu.make_async_copy(tiles[0], held.at[d % 2], sems.at[d % 2]).wait()
        for j in range(0, STEP, 2):
            both = jnp.concatenate([held[d % 2, j], held[d % 2, j + 1]], axis=1)
            raw = jnp.dot(weight_ref[...], both, preferred_element_type=jnp.float32)
            gated = 1.0 / (1.0 + jnp.exp(-(raw + offset_ref[...])))
            result = jnp.where(gate_ref[...] > 0.0, gated, raw).astype(jnp.bfloat16)
            for e in range(CORES):
                for jj in range(2):
                    outs[d][e, j + jj] = result[e * group : (e + 1) * group, jj * lanes : (jj + 1) * lanes]


def project_call(where, weight, offset, gate, tiles, parts):
    line = (len(tiles) + 1) // 2
    channels, lanes = tiles[0].shape[1:]
    group = weight.shape[0] // CORES
    whole = pl.BlockSpec(memory_space=pltpu.VMEM)
    far = pl.BlockSpec(memory_space=pl.ANY)
    shape = jax.ShapeDtypeStruct((CORES, STEP, group, lanes), jnp.bfloat16)
    return pl.pallas_call(
        functools.partial(project_kernel, line, parts),
        in_specs=[pl.BlockSpec(memory_space=pltpu.SMEM), whole, whole, whole, *[far] * len(tiles)],
        out_specs=[whole] * parts,
        out_shape=[shape] * parts,
        scratch_shapes=[
            pltpu.VMEM((2, STEP, channels, lanes), jnp.bfloat16),
            pltpu.SemaphoreType.DMA((2,)),
        ],
        compiler_params=pltpu.CompilerParams(vmem_limit_bytes=VMEM_LIMIT),
        cost_estimate=pl.CostEstimate(
            flops=2 * parts * STEP * channels * lanes * weight.shape[0],
            bytes_accessed=4 * 2**20,
            transcendentals=0,
        ),
        name="project",
    )(where, weight, offset, gate, *tiles)


def place_kernel(parts, part, tile_cols, where_ref, *refs):
    pieces = refs[:parts]
    out_ref, other_ref, rows, sem = refs[-4:]
    mine, core = where_ref[0], where_ref[2]
    step, group, lanes = pieces[0].shape[1:]
    for e, target in enumerate((rows, other_ref)):
        for d in range(parts):
            column = pl.multiple_of((mine ^ d) * lanes, lanes)
            target[:, :, pl.ds(column, lanes)] = pieces[d][e]
        if e == 0:
            row = pl.multiple_of(core * tile_cols + part * step, step)
            copy = pltpu.make_async_copy(rows, out_ref.at[pl.ds(row, step)], sem)
            copy.start()
    copy.wait()


def place_call(where, pieces, earlier, part, parts, tile_cols):
    step, group, lanes = pieces[0].shape[1:]
    far = pl.BlockSpec(memory_space=pl.ANY)
    whole = pl.BlockSpec(memory_space=pltpu.VMEM)
    args = [where, *pieces]
    specs = [pl.BlockSpec(memory_space=pltpu.SMEM), *[whole] * len(pieces)]
    aliases = {}
    if earlier is not None:
        aliases = {len(args): 0}
        args.append(earlier)
        specs.append(far)
    block = (step, group, parts * lanes)
    return pl.pallas_call(
        functools.partial(place_kernel, parts, part, tile_cols),
        in_specs=specs,
        out_specs=(far, whole),
        out_shape=(
            jax.ShapeDtypeStruct((CORES * tile_cols, *block[1:]), jnp.bfloat16),
            jax.ShapeDtypeStruct(block, jnp.bfloat16),
        ),
        scratch_shapes=[pltpu.VMEM(block, jnp.bfloat16), pltpu.SemaphoreType.DMA],
        input_output_aliases=aliases,
        compiler_params=pltpu.CompilerParams(vmem_limit_bytes=VMEM_LIMIT),
        cost_estimate=pl.CostEstimate(flops=0, bytes_accessed=6 * 2**20, transcendentals=0),
        name="place",
    )(*args)


def put_kernel(tile_cols, where_ref, *refs):
    out_ref, sems = refs[-2:]
    copies = []
    for part, rows_ref in enumerate(refs[:-3]):
        step = rows_ref.shape[0]
        row = pl.multiple_of((1 - where_ref[2]) * tile_cols + part * step, step)
        copy = pltpu.make_async_copy(rows_ref, out_ref.at[pl.ds(row, step)], sems.at[part])
        copy.start()
        copies.append(copy)
    for copy in copies:
        copy.wait()


def put_call(where, rows, earlier, tile_cols):
    far = pl.BlockSpec(memory_space=pl.ANY)
    whole = pl.BlockSpec(memory_space=pltpu.VMEM)
    return pl.pallas_call(
        functools.partial(put_kernel, tile_cols),
        in_specs=[pl.BlockSpec(memory_space=pltpu.SMEM), *[whole] * len(rows), far],
        out_specs=far,
        out_shape=jax.ShapeDtypeStruct(earlier.shape, earlier.dtype),
        scratch_shapes=[pltpu.SemaphoreType.DMA((len(rows),))],
        input_output_aliases={1 + len(rows): 0},
        compiler_params=pltpu.CompilerParams(vmem_limit_bytes=VMEM_LIMIT),
        cost_estimate=pl.CostEstimate(flops=0, bytes_accessed=8 * 2**20, transcendentals=0),
        name="put",
    )(where, *rows, earlier)


def shards(
    alignment_left,
    alignment_right,
    pair_features,
    output_weight,
    output_bias,
    norm_scale_gain,
    projection_weight,
    gate_offset_bias,
):
    parts, cols = lax.axis_size("row"), lax.axis_size("col")
    line = cols // CORES
    assert line == parts
    tile_rows, tile_cols, channels = pair_features.shape
    row, col = lax.axis_index("row"), lax.axis_index("col")
    where = jnp.stack([row, col // CORES, col % CORES]).astype(jnp.int32)

    rights = [alignment_right]
    for d in range(1, parts):
        rights.append(lax.ppermute(alignment_right, "row", [(a, a ^ d) for a in range(parts)]))

    ring = [z * CORES for z in range(line)] + [z * CORES + 1 for z in reversed(range(line))]
    onward = [(ring[t], ring[(t + 1) % cols]) for t in range(cols)]
    back = [(b, a) for a, b in onward]

    if alignment_left.shape[0] % 16 == 0:
        held = {0: alignment_left}
        for s in range(1, line):
            ahead, behind = held[-(s - 1)], held[s - 1]
            if s == line - 1:
                ahead, behind, _ = lax.optimization_barrier((ahead, behind, rights[1:]))
            held[-s] = lax.ppermute(ahead, "col", onward)
            held[s] = lax.ppermute(behind, "col", back)
        half = alignment_left.shape[1] // 2
        plan = tuple((offset, 0) for offset in sorted(held)) + ((line, 0), (line, half))
        lefts = [held[offset] for offset in sorted(held)]
        lefts.append(lax.ppermute(held[1 - line][:, :half], "col", onward))
        lefts.append(lax.ppermute(held[line - 1][:, half:], "col", back))
    else:
        plan = ((None, 0),)
        lefts = [lax.all_gather(alignment_left, "col", axis=0, tiled=True)]

    weight = output_weight.T
    bias = output_bias.reshape(channels, 1)
    gain = norm_scale_gain.reshape(channels, 1)

    total = projection_weight.shape[1]
    group = total // cols
    gate_start = total - gate_offset_bias.shape[0]
    turned = projection_weight.T
    offsets = jnp.concatenate([jnp.zeros((gate_start,), jnp.float32), gate_offset_bias]).reshape(total, 1)
    gates = (jnp.arange(total) >= gate_start).astype(jnp.float32).reshape(total, 1)

    def chosen(array):
        return jnp.concatenate(
            [lax.dynamic_slice_in_dim(array, (col ^ e) * group, group, 0) for e in range(CORES)], axis=0
        )

    my_weight, my_offsets, my_gates = chosen(turned), chosen(offsets), chosen(gates)

    count = tile_cols // STEP
    state = {"new_pair": None, "result": None}
    tiles = [{} for _ in range(count)]
    moved = [None] * count
    handed = [None] * count

    def after(value, *others):
        return lax.optimization_barrier((value, others))[0]

    def update(part, *others):
        state["new_pair"], tiles[part][0] = update_call(
            after(where, *others),
            lefts,
            plan,
            cols,
            rights,
            pair_features,
            weight,
            bias,
            gain,
            state["new_pair"],
            part,
        )

    def shift(part, s, *others):
        here = tiles[part]
        here[-s] = lax.ppermute(after(here[-(s - 1)], *others), "col", onward)
        here[s] = lax.ppermute(after(here[s - 1], *others), "col", back)

    def project(part, *others):
        here = tiles[part]
        moved[part] = list(
            project_call(
                after(where, *others),
                my_weight,
                my_offsets,
                my_gates,
                [here[o] for o in range(-(line - 1), line)],
                parts,
            )
        )

    def send(part, d, *others):
        piece = after(moved[part][d], *others)
        moved[part][d] = lax.ppermute(piece, "row", [(a, a ^ d) for a in range(parts)])

    def place(part, *others):
        state["result"], handed[part] = place_call(
            after(where, *others), moved[part], state["result"], part, parts, tile_cols
        )

    def exchange(part, *others):
        handed[part] = after(handed[part], *others)
        swapped[part] = lax.ppermute(handed[part], "col", [(c, c ^ 1) for c in range(cols)])

    order = sorted(
        ((part, s) for part in range(count) for s in range(1, line)),
        key=lambda step: (step[0] + step[1], step[0]),
    )
    first = [order.index((part, 1)) for part in range(count)]
    last = [order.index((part, line - 1)) for part in range(count)]
    gates = [[] for _ in range(len(order) + 2)]
    swapped = [None] * count
    done = []

    update(0, my_weight, my_offsets, my_gates)
    for index, (part, s) in enumerate(order):
        shift(part, s, *gates[index])
        done.append([tiles[part][-s], tiles[part][s]])
        gates[index + 2] += done[index]
        before = done[index - 1] if index else []
        for p in range(1, count):
            if index == max(0, first[p] - 2):
                update(p, *before)
                gates[index + 2].append(tiles[p][0])
        for p in range(count - 1):
            if index == last[p] + 1:
                project(p, *before, *(moved[p - 1][1:] if p else []))
                gates[min(index + 2, len(order) - 1)].append(moved[p][0])
            for d in range(1, parts):
                if index == last[p] + d and p < count - 2:
                    send(p, d, *before)
                    gates[index + 2].append(moved[p][d])
            if p < count - 2 and index == min(last[p] + parts + 1, len(order) - 1):
                place(p, *before)
                gates[min(index + 2, len(order) - 1)].append(handed[p])
    for d in range(1, parts):
        send(count - 2, d, *(moved[count - 2][1:3] if d > 2 else []))
    project(count - 1, *moved[count - 2][1:])
    for d in range(1, parts):
        send(count - 1, d)
    place(count - 2)
    place(count - 1, *handed[:-1])
    for part in range(count):
        exchange(part, *moved[-1][1:])
    state["result"] = put_call(where, swapped, state["result"], tile_cols)
    return (state["new_pair"], state["result"])


def solution(mesh):
    placed = (
        P(("row", "col"), None),
        P("row", "col"),
        P("row", "col", None),
        P(),
        P(),
        P(),
        P(),
        P(),
    )
    return jax.shard_map(
        shards,
        mesh=mesh,
        in_specs=placed,
        out_specs=(P("row", "col", None), P("row", "col", None)),
        check_vma=False,
    )
```

```python
import functools

import jax
import jax.numpy as jnp
from jax import lax
from jax.experimental import pallas as pl
from jax.experimental.pallas import tpu as pltpu
from jax.sharding import PartitionSpec as P

CHANNEL_WIDTH = 32
CORES = 2
STEP = 16
VMEM_LIMIT = 50 * 1024 * 1024

norm_eps = 1e-05

NT = (((1,), (1,)), ((), ()))


def update_kernel(
    parts,
    part,
    cols,
    plan,
    where_ref,
    *refs,
):
    lefts, refs = refs[: len(plan)], refs[len(plan) :]
    rights = refs[:parts]
    pair_ref, weight_ref, bias_ref, gain_ref = refs[parts : parts + 4]
    new_ref, normed_ref, left_ref, right_all, right_turned, outer, rows, sems = refs[-8:]
    tile_rows = pair_ref.shape[0]
    share = rights[0].shape[0]
    depth = share * parts
    width = STEP * CHANNEL_WIDTH
    mine = where_ref[0]
    copies = []
    for d in range(parts):
        source = rights[d].at[:, pl.ds(part * width, width)]
        place = pl.multiple_of((mine ^ d) * share, share)
        copy = pltpu.make_async_copy(source, right_all.at[pl.ds(place, share), :], sems.at[d])
        copy.start()
        copies.append(copy)
    chip, core = where_ref[1], where_ref[2]
    spot = chip + core * (cols - 1 - 2 * chip)
    for n, (offset, column) in enumerate(plan):
        height, length = lefts[n].shape
        row = 0
        if offset is not None:
            owner = lax.rem(spot + offset + cols, cols)
            owner = jnp.where(owner < cols // 2, CORES * owner, CORES * (cols - 1 - owner) + 1)
            row = pl.multiple_of(owner * height, height)
        target = left_ref.at[pl.ds(row, height), pl.ds(column, length)]
        copy = pltpu.make_async_copy(lefts[n], target, sems.at[parts + n])
        copy.start()
        copies.append(copy)
    rows[...] = pair_ref[...].astype(jnp.float32).reshape(tile_rows * STEP, -1)
    for copy in copies[:parts]:
        copy.wait()
    right_turned[...] = right_all[...].T
    for copy in copies[parts:]:
        copy.wait()
    for c1 in range(0, CHANNEL_WIDTH, 2):
        both = jnp.concatenate(
            [left_ref[:, c * depth : (c + 1) * depth] for c in (c1, c1 + 1)], axis=0
        )
        product = lax.dot_general(right_turned[...], both, NT, preferred_element_type=jnp.float32)
        outer[:, c1 * tile_rows : (c1 + 2) * tile_rows] = (product * (1.0 / depth)).astype(jnp.bfloat16)
    for j in range(0, STEP, 2):
        columns = [
            jnp.concatenate(
                [
                    outer[
                        jj * CHANNEL_WIDTH : (jj + 1) * CHANNEL_WIDTH,
                        c1 * tile_rows : (c1 + 1) * tile_rows,
                    ]
                    for c1 in range(CHANNEL_WIDTH)
                ],
                axis=0,
            )
            for jj in (j, j + 1)
        ]
        update = jnp.dot(
            weight_ref[...], jnp.concatenate(columns, axis=1), preferred_element_type=jnp.float32
        )
        for jj in (j, j + 1):
            mine_update = update[:, (jj - j) * tile_rows : (jj - j + 1) * tile_rows] + bias_ref[...]
            place = pl.ds(jj, tile_rows, stride=STEP)
            fresh = rows[place, :].T + mine_update
            widened = fresh.astype(jnp.bfloat16).astype(jnp.float32)
            rows[place, :] = widened.T
            centred = widened - jnp.mean(widened, axis=0, keepdims=True)
            variance = jnp.mean(centred * centred, axis=0, keepdims=True)
            normed_ref[jj] = (centred * lax.rsqrt(variance + norm_eps) * gain_ref[...]).astype(jnp.bfloat16)
    new_ref[...] = rows[...].reshape(tile_rows, STEP, -1).astype(jnp.bfloat16)


def update_call(where, lefts, plan, cols, rights, pair, weight, bias, gain, earlier, part):
    tile_rows, tile_cols, channels = pair.shape
    parts = len(rights)
    depth = rights[0].shape[0] * parts
    width = STEP * CHANNEL_WIDTH
    whole = pl.BlockSpec(memory_space=pltpu.VMEM)
    far = pl.BlockSpec(memory_space=pl.ANY)
    block = pl.BlockSpec((tile_rows, STEP, channels), lambda g: (0, part, 0))
    args = [where, *lefts, *rights, pair, weight, bias, gain]
    specs = [
        pl.BlockSpec(memory_space=pltpu.SMEM),
        *[far] * (len(lefts) + parts),
        block,
        whole,
        whole,
        whole,
    ]
    aliases = {}
    if earlier is not None:
        aliases = {len(args): 0}
        args.append(earlier)
        specs.append(far)
    flops = 2 * width * CHANNEL_WIDTH * tile_rows * depth + 2 * STEP * tile_rows * CHANNEL_WIDTH**2 * channels
    return pl.pallas_call(
        functools.partial(update_kernel, parts, part, cols, plan),
        grid=(1,),
        in_specs=specs,
        out_specs=(block, pl.BlockSpec((STEP, channels, tile_rows), lambda g: (0, 0, 0))),
        out_shape=(
            jax.ShapeDtypeStruct(pair.shape, jnp.bfloat16),
            jax.ShapeDtypeStruct((STEP, channels, tile_rows), jnp.bfloat16),
        ),
        scratch_shapes=[
            pltpu.VMEM((tile_rows, CHANNEL_WIDTH * depth), jnp.bfloat16),
            pltpu.VMEM((depth, width), jnp.bfloat16),
            pltpu.VMEM((width, depth), jnp.bfloat16),
            pltpu.VMEM((width, CHANNEL_WIDTH * tile_rows), jnp.bfloat16),
            pltpu.VMEM((tile_rows * STEP, channels), jnp.float32),
            pltpu.SemaphoreType.DMA((parts + len(plan),)),
        ],
        input_output_aliases=aliases,
        compiler_params=pltpu.CompilerParams(vmem_limit_bytes=VMEM_LIMIT),
        cost_estimate=pl.CostEstimate(flops=flops, bytes_accessed=8 * 2**20, transcendentals=0),
        name="update",
    )(*args)


def project_kernel(line, parts, where_ref, weight_ref, offset_ref, gate_ref, *refs):
    tiles = refs[: 2 * line - 1]
    outs = refs[2 * line - 1 : 2 * line - 1 + parts]
    held, sems = refs[-2:]
    mine, place, core = where_ref[0], where_ref[1], where_ref[2]
    group = weight_ref.shape[0] // CORES
    lanes = held.shape[-1]

    def fetch(d):
        distance = ((mine ^ d) - place) * (1 - 2 * core)
        for index in range(2 * line - 1):
            @pl.when(distance == index - (line - 1))
            def _():
                pltpu.make_async_copy(tiles[index], held.at[d % 2], sems.at[d % 2]).start()

    fetch(0)
    for d in range(parts):
        if d + 1 < parts:
            fetch(d + 1)
        pltpu.make_async_copy(tiles[0], held.at[d % 2], sems.at[d % 2]).wait()
        for j in range(0, STEP, 2):
            both = jnp.concatenate([held[d % 2, j], held[d % 2, j + 1]], axis=1)
            raw = jnp.dot(weight_ref[...], both, preferred_element_type=jnp.float32)
            gated = 1.0 / (1.0 + jnp.exp(-(raw + offset_ref[...])))
            result = jnp.where(gate_ref[...] > 0.0, gated, raw).astype(jnp.bfloat16)
            for e in range(CORES):
                for jj in range(2):
                    outs[d][e, j + jj] = result[e * group : (e + 1) * group, jj * lanes : (jj + 1) * lanes]


def project_call(where, weight, offset, gate, tiles, parts):
    line = (len(tiles) + 1) // 2
    channels, lanes = tiles[0].shape[1:]
    group = weight.shape[0] // CORES
    whole = pl.BlockSpec(memory_space=pltpu.VMEM)
    far = pl.BlockSpec(memory_space=pl.ANY)
    shape = jax.ShapeDtypeStruct((CORES, STEP, group, lanes), jnp.bfloat16)
    return pl.pallas_call(
        functools.partial(project_kernel, line, parts),
        in_specs=[pl.BlockSpec(memory_space=pltpu.SMEM), whole, whole, whole, *[far] * len(tiles)],
        out_specs=[whole] * parts,
        out_shape=[shape] * parts,
        scratch_shapes=[
            pltpu.VMEM((2, STEP, channels, lanes), jnp.bfloat16),
            pltpu.SemaphoreType.DMA((2,)),
        ],
        compiler_params=pltpu.CompilerParams(vmem_limit_bytes=VMEM_LIMIT),
        cost_estimate=pl.CostEstimate(
            flops=2 * parts * STEP * channels * lanes * weight.shape[0],
            bytes_accessed=4 * 2**20,
            transcendentals=0,
        ),
        name="project",
    )(where, weight, offset, gate, *tiles)


def place_kernel(parts, part, tile_cols, where_ref, *refs):
    pieces = refs[:parts]
    out_ref, other_ref, rows, sem = refs[-4:]
    mine, core = where_ref[0], where_ref[2]
    step, group, lanes = pieces[0].shape[1:]
    for e, target in enumerate((rows, other_ref)):
        for d in range(parts):
            column = pl.multiple_of((mine ^ d) * lanes, lanes)
            target[:, :, pl.ds(column, lanes)] = pieces[d][e]
        if e == 0:
            row = pl.multiple_of(core * tile_cols + part * step, step)
            copy = pltpu.make_async_copy(rows, out_ref.at[pl.ds(row, step)], sem)
            copy.start()
    copy.wait()


def place_call(where, pieces, earlier, part, parts, tile_cols):
    step, group, lanes = pieces[0].shape[1:]
    far = pl.BlockSpec(memory_space=pl.ANY)
    whole = pl.BlockSpec(memory_space=pltpu.VMEM)
    args = [where, *pieces]
    specs = [pl.BlockSpec(memory_space=pltpu.SMEM), *[whole] * len(pieces)]
    aliases = {}
    if earlier is not None:
        aliases = {len(args): 0}
        args.append(earlier)
        specs.append(far)
    block = (step, group, parts * lanes)
    return pl.pallas_call(
        functools.partial(place_kernel, parts, part, tile_cols),
        in_specs=specs,
        out_specs=(far, whole),
        out_shape=(
            jax.ShapeDtypeStruct((CORES * tile_cols, *block[1:]), jnp.bfloat16),
            jax.ShapeDtypeStruct(block, jnp.bfloat16),
        ),
        scratch_shapes=[pltpu.VMEM(block, jnp.bfloat16), pltpu.SemaphoreType.DMA],
        input_output_aliases=aliases,
        compiler_params=pltpu.CompilerParams(vmem_limit_bytes=VMEM_LIMIT),
        cost_estimate=pl.CostEstimate(flops=0, bytes_accessed=6 * 2**20, transcendentals=0),
        name="place",
    )(*args)


def put_kernel(owners, tile_cols, where_ref, *refs):
    out_ref, sems = refs[-2:]
    copies = []
    for n, rows_ref in enumerate(refs[:-3]):
        step = rows_ref.shape[0]
        row = pl.multiple_of((1 - where_ref[2]) * tile_cols + owners[n] * step, step)
        copy = pltpu.make_async_copy(rows_ref, out_ref.at[pl.ds(row, step)], sems.at[n])
        copy.start()
        copies.append(copy)
    for copy in copies:
        copy.wait()


def put_call(where, owners, rows, earlier, tile_cols):
    far = pl.BlockSpec(memory_space=pl.ANY)
    whole = pl.BlockSpec(memory_space=pltpu.VMEM)
    return pl.pallas_call(
        functools.partial(put_kernel, tuple(owners), tile_cols),
        in_specs=[pl.BlockSpec(memory_space=pltpu.SMEM), *[whole] * len(rows), far],
        out_specs=far,
        out_shape=jax.ShapeDtypeStruct(earlier.shape, earlier.dtype),
        scratch_shapes=[pltpu.SemaphoreType.DMA((len(rows),))],
        input_output_aliases={1 + len(rows): 0},
        compiler_params=pltpu.CompilerParams(vmem_limit_bytes=VMEM_LIMIT),
        cost_estimate=pl.CostEstimate(flops=0, bytes_accessed=8 * 2**20, transcendentals=0),
        name="put",
    )(where, *rows, earlier)


def shards(
    alignment_left,
    alignment_right,
    pair_features,
    output_weight,
    output_bias,
    norm_scale_gain,
    projection_weight,
    gate_offset_bias,
):
    parts, cols = lax.axis_size("row"), lax.axis_size("col")
    line = cols // CORES
    assert line == parts
    tile_rows, tile_cols, channels = pair_features.shape
    row, col = lax.axis_index("row"), lax.axis_index("col")
    where = jnp.stack([row, col // CORES, col % CORES]).astype(jnp.int32)

    rights = [alignment_right]
    for d in range(1, parts):
        rights.append(lax.ppermute(alignment_right, "row", [(a, a ^ d) for a in range(parts)]))

    ring = [z * CORES for z in range(line)] + [z * CORES + 1 for z in reversed(range(line))]
    onward = [(ring[t], ring[(t + 1) % cols]) for t in range(cols)]
    back = [(b, a) for a, b in onward]

    if alignment_left.shape[0] % 16 == 0:
        held = {0: alignment_left}
        for s in range(1, line):
            ahead, behind = held[-(s - 1)], held[s - 1]
            if s == line - 1:
                ahead, behind, _ = lax.optimization_barrier((ahead, behind, rights[1:]))
            held[-s] = lax.ppermute(ahead, "col", onward)
            held[s] = lax.ppermute(behind, "col", back)
        half = alignment_left.shape[1] // 2
        plan = tuple((offset, 0) for offset in sorted(held)) + ((line, 0), (line, half))
        lefts = [held[offset] for offset in sorted(held)]
        lefts.append(lax.ppermute(held[1 - line][:, :half], "col", onward))
        lefts.append(lax.ppermute(held[line - 1][:, half:], "col", back))
    else:
        plan = ((None, 0),)
        lefts = [lax.all_gather(alignment_left, "col", axis=0, tiled=True)]

    weight = output_weight.T
    bias = output_bias.reshape(channels, 1)
    gain = norm_scale_gain.reshape(channels, 1)

    total = projection_weight.shape[1]
    group = total // cols
    gate_start = total - gate_offset_bias.shape[0]
    turned = projection_weight.T
    offsets = jnp.concatenate([jnp.zeros((gate_start,), jnp.float32), gate_offset_bias]).reshape(total, 1)
    gates = (jnp.arange(total) >= gate_start).astype(jnp.float32).reshape(total, 1)

    def chosen(array):
        return jnp.concatenate(
            [lax.dynamic_slice_in_dim(array, (col ^ e) * group, group, 0) for e in range(CORES)], axis=0
        )

    my_weight, my_offsets, my_gates = chosen(turned), chosen(offsets), chosen(gates)

    count = tile_cols // STEP
    state = {"new_pair": None, "result": None}
    tiles = [{} for _ in range(count)]
    moved = [None] * count
    handed = [None] * count

    def after(value, *others):
        return lax.optimization_barrier((value, others))[0]

    def update(part, *others):
        state["new_pair"], tiles[part][0] = update_call(
            after(where, *others),
            lefts,
            plan,
            cols,
            rights,
            pair_features,
            weight,
            bias,
            gain,
            state["new_pair"],
            part,
        )

    def shift(part, s, *others):
        here = tiles[part]
        here[-s] = lax.ppermute(after(here[-(s - 1)], *others), "col", onward)
        here[s] = lax.ppermute(after(here[s - 1], *others), "col", back)

    def project(part, *others):
        here = tiles[part]
        moved[part] = list(
            project_call(
                after(where, *others),
                my_weight,
                my_offsets,
                my_gates,
                [here[o] for o in range(-(line - 1), line)],
                parts,
            )
        )

    def send(part, d, *others):
        piece = after(moved[part][d], *others)
        moved[part][d] = lax.ppermute(piece, "row", [(a, a ^ d) for a in range(parts)])

    def place(part, *others):
        state["result"], handed[part] = place_call(
            after(where, *others), moved[part], state["result"], part, parts, tile_cols
        )

    def exchange(part, *others):
        handed[part] = after(handed[part], *others)
        swapped[part] = lax.ppermute(handed[part], "col", [(c, c ^ 1) for c in range(cols)])

    order = sorted(
        ((part, s) for part in range(count) for s in range(1, line)),
        key=lambda step: (step[0] + step[1], step[0]),
    )
    first = [order.index((part, 1)) for part in range(count)]
    last = [order.index((part, line - 1)) for part in range(count)]
    gates = [[] for _ in range(len(order) + 2)]
    swapped = [None] * count
    done = []

    update(0, my_weight, my_offsets, my_gates)
    for index, (part, s) in enumerate(order):
        shift(part, s, *gates[index])
        done.append([tiles[part][-s], tiles[part][s]])
        gates[index + 2] += done[index]
        before = done[index - 1] if index else []
        for p in range(1, count):
            if index == max(0, first[p] - 2):
                update(p, *before)
                gates[index + 2].append(tiles[p][0])
        for p in range(count - 1):
            if index == last[p] + 1:
                project(p, *before, *(moved[p - 1][1:] if p else []))
                gates[min(index + 2, len(order) - 1)].append(moved[p][0])
            for d in range(1, parts):
                if index == last[p] + d and p < count - 2:
                    send(p, d, *before)
                    gates[index + 2].append(moved[p][d])
            if p < count - 2 and index == min(last[p] + parts + 1, len(order) - 1):
                place(p, *before)
                gates[min(index + 2, len(order) - 1)].append(handed[p])
    for d in range(1, parts):
        send(count - 2, d, *(done[-2] if d > 2 else []))
    project(count - 1, *moved[count - 2][1:])
    for d in range(1, parts):
        send(count - 1, d)
    place(count - 2)
    place(count - 1, *handed[:-1])
    for part in range(count):
        exchange(part, *(moved[-1][1:] if part >= count - 2 else moved[-1][:1]))
    state["result"] = put_call(where, range(count), swapped, state["result"], tile_cols)
    return (state["new_pair"], state["result"])


def solution(mesh):
    placed = (
        P(("row", "col"), None),
        P("row", "col"),
        P("row", "col", None),
        P(),
        P(),
        P(),
        P(),
        P(),
    )
    return jax.shard_map(
        shards,
        mesh=mesh,
        in_specs=placed,
        out_specs=(P("row", "col", None), P("row", "col", None)),
        check_vma=False,
    )
```

```python
import functools

import jax
import jax.numpy as jnp
from jax import lax
from jax.experimental import pallas as pl
from jax.experimental.pallas import tpu as pltpu
from jax.sharding import PartitionSpec as P

CHANNEL_WIDTH = 32
CORES = 2
STEP = 16
VMEM_LIMIT = 50 * 1024 * 1024

norm_eps = 1e-05

NT = (((1,), (1,)), ((), ()))


def update_kernel(
    parts,
    part,
    cols,
    plan,
    where_ref,
    *refs,
):
    lefts, refs = refs[: len(plan)], refs[len(plan) :]
    rights = refs[:parts]
    pair_ref, weight_ref, bias_ref, gain_ref = refs[parts : parts + 4]
    new_ref, normed_ref, left_ref, right_all, right_turned, outer, rows, sems = refs[-8:]
    tile_rows = pair_ref.shape[0]
    share = rights[0].shape[0]
    depth = share * parts
    width = STEP * CHANNEL_WIDTH
    mine = where_ref[0]
    copies = []
    for d in range(parts):
        source = rights[d].at[:, pl.ds(part * width, width)]
        place = pl.multiple_of((mine ^ d) * share, share)
        copy = pltpu.make_async_copy(source, right_all.at[pl.ds(place, share), :], sems.at[d])
        copy.start()
        copies.append(copy)
    chip, core = where_ref[1], where_ref[2]
    spot = chip + core * (cols - 1 - 2 * chip)
    for n, (offset, column) in enumerate(plan):
        height, length = lefts[n].shape
        row = 0
        if offset is not None:
            owner = lax.rem(spot + offset + cols, cols)
            owner = jnp.where(owner < cols // 2, CORES * owner, CORES * (cols - 1 - owner) + 1)
            row = pl.multiple_of(owner * height, height)
        target = left_ref.at[pl.ds(row, height), pl.ds(column, length)]
        copy = pltpu.make_async_copy(lefts[n], target, sems.at[parts + n])
        copy.start()
        copies.append(copy)
    rows[...] = pair_ref[...].astype(jnp.float32).reshape(tile_rows * STEP, -1)
    for copy in copies[:parts]:
        copy.wait()
    right_turned[...] = right_all[...].T
    for copy in copies[parts:]:
        copy.wait()
    for c1 in range(0, CHANNEL_WIDTH, 2):
        both = jnp.concatenate(
            [left_ref[:, c * depth : (c + 1) * depth] for c in (c1, c1 + 1)], axis=0
        )
        product = lax.dot_general(right_turned[...], both, NT, preferred_element_type=jnp.float32)
        outer[:, c1 * tile_rows : (c1 + 2) * tile_rows] = (product * (1.0 / depth)).astype(jnp.bfloat16)
    for j in range(0, STEP, 2):
        columns = [
            jnp.concatenate(
                [
                    outer[
                        jj * CHANNEL_WIDTH : (jj + 1) * CHANNEL_WIDTH,
                        c1 * tile_rows : (c1 + 1) * tile_rows,
                    ]
                    for c1 in range(CHANNEL_WIDTH)
                ],
                axis=0,
            )
            for jj in (j, j + 1)
        ]
        update = jnp.dot(
            weight_ref[...], jnp.concatenate(columns, axis=1), preferred_element_type=jnp.float32
        )
        for jj in (j, j + 1):
            mine_update = update[:, (jj - j) * tile_rows : (jj - j + 1) * tile_rows] + bias_ref[...]
            place = pl.ds(jj, tile_rows, stride=STEP)
            fresh = rows[place, :].T + mine_update
            widened = fresh.astype(jnp.bfloat16).astype(jnp.float32)
            rows[place, :] = widened.T
            centred = widened - jnp.mean(widened, axis=0, keepdims=True)
            variance = jnp.mean(centred * centred, axis=0, keepdims=True)
            normed_ref[jj] = (centred * lax.rsqrt(variance + norm_eps) * gain_ref[...]).astype(jnp.bfloat16)
    new_ref[...] = rows[...].reshape(tile_rows, STEP, -1).astype(jnp.bfloat16)


def update_call(where, lefts, plan, cols, rights, pair, weight, bias, gain, earlier, part):
    tile_rows, tile_cols, channels = pair.shape
    parts = len(rights)
    depth = rights[0].shape[0] * parts
    width = STEP * CHANNEL_WIDTH
    whole = pl.BlockSpec(memory_space=pltpu.VMEM)
    far = pl.BlockSpec(memory_space=pl.ANY)
    block = pl.BlockSpec((tile_rows, STEP, channels), lambda g: (0, part, 0))
    args = [where, *lefts, *rights, pair, weight, bias, gain]
    specs = [
        pl.BlockSpec(memory_space=pltpu.SMEM),
        *[far] * (len(lefts) + parts),
        block,
        whole,
        whole,
        whole,
    ]
    aliases = {}
    if earlier is not None:
        aliases = {len(args): 0}
        args.append(earlier)
        specs.append(far)
    flops = 2 * width * CHANNEL_WIDTH * tile_rows * depth + 2 * STEP * tile_rows * CHANNEL_WIDTH**2 * channels
    return pl.pallas_call(
        functools.partial(update_kernel, parts, part, cols, plan),
        grid=(1,),
        in_specs=specs,
        out_specs=(block, pl.BlockSpec((STEP, channels, tile_rows), lambda g: (0, 0, 0))),
        out_shape=(
            jax.ShapeDtypeStruct(pair.shape, jnp.bfloat16),
            jax.ShapeDtypeStruct((STEP, channels, tile_rows), jnp.bfloat16),
        ),
        scratch_shapes=[
            pltpu.VMEM((tile_rows, CHANNEL_WIDTH * depth), jnp.bfloat16),
            pltpu.VMEM((depth, width), jnp.bfloat16),
            pltpu.VMEM((width, depth), jnp.bfloat16),
            pltpu.VMEM((width, CHANNEL_WIDTH * tile_rows), jnp.bfloat16),
            pltpu.VMEM((tile_rows * STEP, channels), jnp.float32),
            pltpu.SemaphoreType.DMA((parts + len(plan),)),
        ],
        input_output_aliases=aliases,
        compiler_params=pltpu.CompilerParams(vmem_limit_bytes=VMEM_LIMIT),
        cost_estimate=pl.CostEstimate(flops=flops, bytes_accessed=8 * 2**20, transcendentals=0),
        name="update",
    )(*args)


def project_kernel(line, parts, where_ref, weight_ref, offset_ref, gate_ref, *refs):
    tiles = refs[: 2 * line - 1]
    outs = refs[2 * line - 1 : 2 * line - 1 + parts]
    held, sems = refs[-2:]
    mine, place, core = where_ref[0], where_ref[1], where_ref[2]
    group = weight_ref.shape[0] // CORES
    lanes = held.shape[-1]

    def fetch(d):
        distance = ((mine ^ d) - place) * (1 - 2 * core)
        for index in range(2 * line - 1):
            @pl.when(distance == index - (line - 1))
            def _():
                pltpu.make_async_copy(tiles[index], held.at[d % 2], sems.at[d % 2]).start()

    fetch(0)
    for d in range(parts):
        if d + 1 < parts:
            fetch(d + 1)
        pltpu.make_async_copy(tiles[0], held.at[d % 2], sems.at[d % 2]).wait()
        for j in range(0, STEP, 2):
            both = jnp.concatenate([held[d % 2, j], held[d % 2, j + 1]], axis=1)
            raw = jnp.dot(weight_ref[...], both, preferred_element_type=jnp.float32)
            gated = 1.0 / (1.0 + jnp.exp(-(raw + offset_ref[...])))
            result = jnp.where(gate_ref[...] > 0.0, gated, raw).astype(jnp.bfloat16)
            for e in range(CORES):
                for jj in range(2):
                    outs[d][e, j + jj] = result[e * group : (e + 1) * group, jj * lanes : (jj + 1) * lanes]


def project_call(where, weight, offset, gate, tiles, parts):
    line = (len(tiles) + 1) // 2
    channels, lanes = tiles[0].shape[1:]
    group = weight.shape[0] // CORES
    whole = pl.BlockSpec(memory_space=pltpu.VMEM)
    far = pl.BlockSpec(memory_space=pl.ANY)
    shape = jax.ShapeDtypeStruct((CORES, STEP, group, lanes), jnp.bfloat16)
    return pl.pallas_call(
        functools.partial(project_kernel, line, parts),
        in_specs=[pl.BlockSpec(memory_space=pltpu.SMEM), whole, whole, whole, *[far] * len(tiles)],
        out_specs=[whole] * parts,
        out_shape=[shape] * parts,
        scratch_shapes=[
            pltpu.VMEM((2, STEP, channels, lanes), jnp.bfloat16),
            pltpu.SemaphoreType.DMA((2,)),
        ],
        compiler_params=pltpu.CompilerParams(vmem_limit_bytes=VMEM_LIMIT),
        cost_estimate=pl.CostEstimate(
            flops=2 * parts * STEP * channels * lanes * weight.shape[0],
            bytes_accessed=4 * 2**20,
            transcendentals=0,
        ),
        name="project",
    )(where, weight, offset, gate, *tiles)


def place_kernel(parts, part, tile_cols, where_ref, *refs):
    pieces = refs[:parts]
    out_ref, other_ref, rows, sem = refs[-4:]
    mine, core = where_ref[0], where_ref[2]
    step, group, lanes = pieces[0].shape[1:]
    for e, target in enumerate((rows, other_ref)):
        for d in range(parts):
            column = pl.multiple_of((mine ^ d) * lanes, lanes)
            target[:, :, pl.ds(column, lanes)] = pieces[d][e]
        if e == 0:
            row = pl.multiple_of(core * tile_cols + part * step, step)
            copy = pltpu.make_async_copy(rows, out_ref.at[pl.ds(row, step)], sem)
            copy.start()
    copy.wait()


def place_call(where, pieces, earlier, part, parts, tile_cols):
    step, group, lanes = pieces[0].shape[1:]
    far = pl.BlockSpec(memory_space=pl.ANY)
    whole = pl.BlockSpec(memory_space=pltpu.VMEM)
    args = [where, *pieces]
    specs = [pl.BlockSpec(memory_space=pltpu.SMEM), *[whole] * len(pieces)]
    aliases = {}
    if earlier is not None:
        aliases = {len(args): 0}
        args.append(earlier)
        specs.append(far)
    block = (step, group, parts * lanes)
    return pl.pallas_call(
        functools.partial(place_kernel, parts, part, tile_cols),
        in_specs=specs,
        out_specs=(far, whole),
        out_shape=(
            jax.ShapeDtypeStruct((CORES * tile_cols, *block[1:]), jnp.bfloat16),
            jax.ShapeDtypeStruct(block, jnp.bfloat16),
        ),
        scratch_shapes=[pltpu.VMEM(block, jnp.bfloat16), pltpu.SemaphoreType.DMA],
        input_output_aliases=aliases,
        compiler_params=pltpu.CompilerParams(vmem_limit_bytes=VMEM_LIMIT),
        cost_estimate=pl.CostEstimate(flops=0, bytes_accessed=6 * 2**20, transcendentals=0),
        name="place",
    )(*args)


def put_kernel(owners, tile_cols, where_ref, *refs):
    out_ref, sems = refs[-2:]
    copies = []
    for n, rows_ref in enumerate(refs[:-3]):
        step = rows_ref.shape[0]
        row = pl.multiple_of((1 - where_ref[2]) * tile_cols + owners[n] * step, step)
        copy = pltpu.make_async_copy(rows_ref, out_ref.at[pl.ds(row, step)], sems.at[n])
        copy.start()
        copies.append(copy)
    for copy in copies:
        copy.wait()


def put_call(where, owners, rows, earlier, tile_cols):
    far = pl.BlockSpec(memory_space=pl.ANY)
    whole = pl.BlockSpec(memory_space=pltpu.VMEM)
    return pl.pallas_call(
        functools.partial(put_kernel, tuple(owners), tile_cols),
        in_specs=[pl.BlockSpec(memory_space=pltpu.SMEM), *[whole] * len(rows), far],
        out_specs=far,
        out_shape=jax.ShapeDtypeStruct(earlier.shape, earlier.dtype),
        scratch_shapes=[pltpu.SemaphoreType.DMA((len(rows),))],
        input_output_aliases={1 + len(rows): 0},
        compiler_params=pltpu.CompilerParams(vmem_limit_bytes=VMEM_LIMIT),
        cost_estimate=pl.CostEstimate(flops=0, bytes_accessed=8 * 2**20, transcendentals=0),
        name="put",
    )(where, *rows, earlier)


def shards(
    alignment_left,
    alignment_right,
    pair_features,
    output_weight,
    output_bias,
    norm_scale_gain,
    projection_weight,
    gate_offset_bias,
):
    parts, cols = lax.axis_size("row"), lax.axis_size("col")
    line = cols // CORES
    assert line == parts
    tile_rows, tile_cols, channels = pair_features.shape
    row, col = lax.axis_index("row"), lax.axis_index("col")
    where = jnp.stack([row, col // CORES, col % CORES]).astype(jnp.int32)

    rights = [alignment_right]
    for d in range(1, parts):
        rights.append(lax.ppermute(alignment_right, "row", [(a, a ^ d) for a in range(parts)]))

    ring = [z * CORES for z in range(line)] + [z * CORES + 1 for z in reversed(range(line))]
    onward = [(ring[t], ring[(t + 1) % cols]) for t in range(cols)]
    back = [(b, a) for a, b in onward]

    if alignment_left.shape[0] % 16 == 0:
        held = {0: alignment_left}
        for s in range(1, line):
            ahead, behind = held[-(s - 1)], held[s - 1]
            if s == line - 1:
                ahead, behind, _ = lax.optimization_barrier((ahead, behind, rights[1:]))
            held[-s] = lax.ppermute(ahead, "col", onward)
            held[s] = lax.ppermute(behind, "col", back)
        half = alignment_left.shape[1] // 2
        plan = tuple((offset, 0) for offset in sorted(held)) + ((line, 0), (line, half))
        lefts = [held[offset] for offset in sorted(held)]
        lefts.append(lax.ppermute(held[1 - line][:, :half], "col", onward))
        lefts.append(lax.ppermute(held[line - 1][:, half:], "col", back))
    else:
        plan = ((None, 0),)
        lefts = [lax.all_gather(alignment_left, "col", axis=0, tiled=True)]

    weight = output_weight.T
    bias = output_bias.reshape(channels, 1)
    gain = norm_scale_gain.reshape(channels, 1)

    total = projection_weight.shape[1]
    group = total // cols
    gate_start = total - gate_offset_bias.shape[0]
    turned = projection_weight.T
    offsets = jnp.concatenate([jnp.zeros((gate_start,), jnp.float32), gate_offset_bias]).reshape(total, 1)
    gates = (jnp.arange(total) >= gate_start).astype(jnp.float32).reshape(total, 1)

    def chosen(array):
        return jnp.concatenate(
            [lax.dynamic_slice_in_dim(array, (col ^ e) * group, group, 0) for e in range(CORES)], axis=0
        )

    my_weight, my_offsets, my_gates = chosen(turned), chosen(offsets), chosen(gates)

    count = tile_cols // STEP
    state = {"new_pair": None, "result": None}
    tiles = [{} for _ in range(count)]
    moved = [None] * count
    handed = [None] * count

    def after(value, *others):
        return lax.optimization_barrier((value, others))[0]

    def update(part, *others):
        state["new_pair"], tiles[part][0] = update_call(
            after(where, *others),
            lefts,
            plan,
            cols,
            rights,
            pair_features,
            weight,
            bias,
            gain,
            state["new_pair"],
            part,
        )

    def shift(part, s, *others):
        here = tiles[part]
        here[-s] = lax.ppermute(after(here[-(s - 1)], *others), "col", onward)
        here[s] = lax.ppermute(after(here[s - 1], *others), "col", back)

    def project(part, *others):
        here = tiles[part]
        moved[part] = list(
            project_call(
                after(where, *others),
                my_weight,
                my_offsets,
                my_gates,
                [here[o] for o in range(-(line - 1), line)],
                parts,
            )
        )

    def send(part, d, *others):
        piece = after(moved[part][d], *others)
        moved[part][d] = lax.ppermute(piece, "row", [(a, a ^ d) for a in range(parts)])

    def place(part, *others):
        state["result"], handed[part] = place_call(
            after(where, *others), moved[part], state["result"], part, parts, tile_cols
        )

    def exchange(part, *others):
        handed[part] = after(handed[part], *others)
        swapped[part] = lax.ppermute(handed[part], "col", [(c, c ^ 1) for c in range(cols)])

    order = sorted(
        ((part, s) for part in range(count) for s in range(1, line)),
        key=lambda step: (step[0] + step[1], step[0]),
    )
    first = [order.index((part, 1)) for part in range(count)]
    last = [order.index((part, line - 1)) for part in range(count)]
    gates = [[] for _ in range(len(order) + 2)]
    swapped = [None] * count
    done = []

    update(0, my_weight, my_offsets, my_gates)
    for index, (part, s) in enumerate(order):
        shift(part, s, *gates[index])
        done.append([tiles[part][-s], tiles[part][s]])
        gates[index + 2] += done[index]
        before = done[index - 1] if index else []
        for p in range(1, count):
            if index == max(0, first[p] - 2):
                update(p, *before)
                gates[index + 2].append(tiles[p][0])
        for p in range(count - 1):
            if index == last[p] + 1:
                project(p, *before, *(moved[p - 1][1:3] if p else []))
                gates[min(index + 2, len(order) - 1)].append(moved[p][0])
            for d in range(1, parts):
                if index == last[p] + d and p < count - 2:
                    send(p, d, *before)
                    gates[index + 2].append(moved[p][d])
            if p < count - 2 and index == min(last[p] + parts + 1, len(order) - 1):
                place(p, *before)
                gates[min(index + 2, len(order) - 1)].append(handed[p])
    for d in range(1, parts):
        send(count - 2, d, *(done[-2] if d > 2 else []))
    project(count - 1, *moved[count - 2][1:])
    for d in range(1, parts):
        send(count - 1, d)
    place(count - 2)
    place(count - 1, *handed[:-1])
    for part in range(count):
        exchange(part, *(moved[-1][1:] if part >= count - 2 else moved[-1][:1]))
    state["result"] = put_call(where, range(count), swapped, state["result"], tile_cols)
    return (state["new_pair"], state["result"])


def solution(mesh):
    placed = (
        P(("row", "col"), None),
        P("row", "col"),
        P("row", "col", None),
        P(),
        P(),
        P(),
        P(),
        P(),
    )
    return jax.shard_map(
        shards,
        mesh=mesh,
        in_specs=placed,
        out_specs=(P("row", "col", None), P("row", "col", None)),
        check_vma=False,
    )
```
